256 devices in a mesh: frame: 32 (over z_hi, y, core), head: 8 (over z_lo, x).
Axes of the slice: x: 4, y: 4, z: 8 (z_hi: 4, z_lo: 2; z = z_hi * 2 + z_lo), core: 2. Of those that a mesh axis runs over, the one named last changes fastest.
Arguments:
- tokens: bfloat16 [32768, 3072], P('frame'), may hold values from -6 to 6
- qkv_weight: bfloat16 [3, 3072, 3072], P(None, None, 'head'), may hold values from -0.109375 to 0.109375
- query_gain: float32 [128], replicated, may hold values from 0.1 to 1.9
- key_gain: float32 [128], replicated, may hold values from 0.1 to 1.9
- labels: int32 [24], P('head'), may hold values from 0 to 1, as said below
- space_mask: int32 [24, 16, 48], P('head'), may hold values from 0 to 1, as said below
- time_mask: int32 [24, 4, 4], P('head'), may hold values from 0 to 1, as said below
Outputs:
- attended: bfloat16 [32768, 3072], P(('frame', 'head'))
The draws below stay inside these ranges and needn't reach their ends.
Inputs may be any that keep to these rules, and one draw needn't show every extreme that they name: `labels`: among heads 3 * j, 3 * j + 1 and 3 * j + 2 exactly one is temporal. space_mask[h, a, 16 + a] = 1 for every head and query block. For each head, at most 8 key blocks of the previous frame (b < 16) are allowed for some query block, and at most 8 of the next frame (b >= 32); some head reaches 8 on each side. time_mask[h, a, a] = 1 for every head and query block.
All inputs are finite; a program needn't handle non-finite values.
Results may differ from the reference program's by a relative error of at most 0.0073.
Values may be sent and summed in bfloat16 or wider, within the bound.
No kernel may reach another device: no remote copies, remote signals or barrier semaphores. Data moves between devices by JAX's collectives and lax.ppermute only.
A program may use at most 128 MiB of HBM per device.

```python
import math
import jax
import jax.numpy as jnp
from jax import lax

D = 3072
HEADS = 24
HEAD_DIM = 128
TOK_FRAME = 1024
STRIP = 8
BLOCK = 64
FRAMES = 32
TOKENS = 32768
QBLOCKS = 16
TBLOCKS = 4
NEAR_MAX = 8


def draw_labels(key, part):
    groups = HEADS // 3
    chosen = jax.random.randint(key, (groups,), 0, 3)
    marks = jnp.arange(3, dtype=jnp.int32)[None, :] == chosen[:, None]
    return marks.astype(jnp.int32).reshape(HEADS)


def draw_space_mask(key, part):
    keys = jax.random.split(jax.random.fold_in(key, 11), 7)
    density = jax.random.randint(keys[0], (HEADS, 1, 1), 2, 9)
    middle = jax.random.randint(keys[1], (HEADS, QBLOCKS, QBLOCKS), 0, 10) < density
    diagonal = jnp.eye(QBLOCKS, dtype=jnp.int32)[None] == 1
    middle = middle | diagonal
    counts = jax.random.randint(keys[2], (2, HEADS), 1, NEAR_MAX + 1)
    fullest = jax.random.randint(keys[3], (2,), 0, HEADS)
    counts = jnp.where(jnp.arange(HEADS, dtype=jnp.int32)[None, :] == fullest[:, None], NEAR_MAX, counts)
    scores = jax.random.randint(keys[4], (2, HEADS, QBLOCKS), 0, 1 << 20) * QBLOCKS + jnp.arange(QBLOCKS, dtype=jnp.int32)
    ranking = jnp.argsort(jnp.argsort(scores, axis=-1), axis=-1)
    column_on = ranking < counts[:, :, None]
    random_live = jax.random.randint(keys[5], (2, HEADS, QBLOCKS, QBLOCKS), 0, 10) < density[None]
    forced_row = jax.random.randint(keys[6], (2, HEADS, QBLOCKS), 0, QBLOCKS)
    row_ids = jnp.arange(QBLOCKS, dtype=jnp.int32)[None, None, :, None]
    forced = row_ids == forced_row[:, :, None, :]
    near = column_on[:, :, None, :] & (random_live | forced)
    whole = jnp.concatenate([near[0], middle, near[1]], axis=2)
    return whole.astype(jnp.int32)


def draw_time_mask(key, part):
    keys = jax.random.split(jax.random.fold_in(key, 23), 2)
    density = jax.random.randint(keys[0], (HEADS, 1, 1), 2, 9)
    live = jax.random.randint(keys[1], (HEADS, TBLOCKS, TBLOCKS), 0, 10) < density
    live = live | (jnp.eye(TBLOCKS, dtype=jnp.int32)[None] == 1)
    return live.astype(jnp.int32)


def shard_levels(stream_key, shape, shards, least, high):
    loudness = 1.0
    for position, blocks in shards:
        heights = jax.random.uniform(jax.random.fold_in(jax.random.fold_in(stream_key, 6), position), (blocks,), jnp.float32, least / len(shards), high / len(shards))
        loudness = loudness * jnp.repeat(jnp.exp(heights), shape[position] // blocks).reshape((-1,) + (1,) * (len(shape) - 1 - position))
    return loudness


def gaussian(rng, dims, scale, most, cuts=(), held_as=jnp.bfloat16):
    values = scale * jax.random.normal(rng, dims, jnp.float32)
    if cuts:
        values = values * shard_levels(rng, dims, cuts, -0.22, 0.18)
    return jnp.clip(values, -most, most).astype(held_as)


def setup_inputs(seed: int = 0) -> dict:
    arg_keys = jax.random.split(jax.random.key(seed), 8)
    tokens = gaussian(arg_keys[0], (TOKENS, D), 1.0, 6.0, ((0, 32),))
    qkv_weight = gaussian(arg_keys[1], (3, D, HEADS * HEAD_DIM), D ** -0.5, 0.109375, ((2, 8),))
    query_gain = jnp.clip(1.0 + 0.18 * jax.random.normal(arg_keys[2], (HEAD_DIM,), jnp.float32), 0.1, 1.9)
    key_gain = jnp.clip(1.0 + 0.18 * jax.random.normal(arg_keys[3], (HEAD_DIM,), jnp.float32), 0.1, 1.9)
    labels = draw_labels(jax.random.fold_in(arg_keys[7], 71), 0)
    space_mask = draw_space_mask(jax.random.fold_in(arg_keys[7], 71), 0)
    time_mask = draw_time_mask(jax.random.fold_in(arg_keys[7], 71), 0)
    return dict(tokens=tokens, qkv_weight=qkv_weight, query_gain=query_gain, key_gain=key_gain, labels=labels, space_mask=space_mask, time_mask=time_mask)


epsilon = 1e-06

def normed(projected, gains):
    inverse_rms = lax.rsqrt(lax.optimization_barrier(jnp.mean(projected * projected, axis=-1, keepdims=True)) + epsilon)
    return (projected * inverse_rms * gains).astype(jnp.bfloat16)

def expand(block_mask):
    widened = jnp.repeat(block_mask.astype(jnp.float32), BLOCK, axis=-2)
    return jnp.repeat(widened, BLOCK, axis=-1)

def attend(queries, key_rows, values, allowed):
    scores = jnp.einsum('...rd,...cd->...rc', queries.astype(jnp.float32), key_rows.astype(jnp.float32)) / math.sqrt(HEAD_DIM)
    weight = jnp.exp(scores) * allowed
    denominator = lax.optimization_barrier(jnp.sum(weight, axis=-1, keepdims=True))
    rounded = lax.optimization_barrier(weight.astype(jnp.bfloat16)).astype(jnp.float32)
    return jnp.einsum('...rc,...cd->...rd', rounded, values.astype(jnp.float32)) / denominator

def space_head(queries, key_rows, values, space_live, time_live):
    blank = jnp.zeros((1, TOK_FRAME, HEAD_DIM), jnp.bfloat16)
    padded_keys = jnp.concatenate([blank, key_rows, blank], axis=0)
    padded_values = jnp.concatenate([blank, values, blank], axis=0)
    window_keys = jnp.concatenate([padded_keys[:-2], padded_keys[1:-1], padded_keys[2:]], axis=1)
    window_values = jnp.concatenate([padded_values[:-2], padded_values[1:-1], padded_values[2:]], axis=1)
    frame_ids = jnp.arange(FRAMES, dtype=jnp.int32)
    lower_ok = (frame_ids > 0).astype(jnp.float32)
    upper_ok = (frame_ids < FRAMES - 1).astype(jnp.float32)
    ones_row = jnp.ones((FRAMES, QBLOCKS), jnp.float32)
    reach = jnp.concatenate([ones_row * lower_ok[:, None], ones_row, ones_row * upper_ok[:, None]], axis=1)

    def one_frame(frame_items):
        frame_q, frame_k, frame_v, frame_reach = frame_items
        allowed = expand(space_live.astype(jnp.float32) * frame_reach[None, :])
        return attend(frame_q, frame_k, frame_v, allowed)
    return lax.map(one_frame, (queries, window_keys, window_values, reach))

def to_strips(whole):
    strip_count = TOK_FRAME // STRIP
    shaped = whole.reshape(FRAMES, strip_count, STRIP, HEAD_DIM).transpose(1, 0, 2, 3)
    return shaped.reshape(strip_count, FRAMES * STRIP, HEAD_DIM)

def time_head(queries, key_rows, values, space_live, time_live):
    strip_count = TOK_FRAME // STRIP
    allowed = expand(time_live)[None]
    result = attend(to_strips(queries), to_strips(key_rows), to_strips(values), allowed)
    result = result.reshape(strip_count, FRAMES, STRIP, HEAD_DIM).transpose(1, 0, 2, 3)
    return result.reshape(FRAMES, TOK_FRAME, HEAD_DIM)

def reference(tokens, qkv_weight, query_gain, key_gain, labels, space_mask, time_mask):

    def project(index):
        product = jnp.dot(tokens, qkv_weight[index], preferred_element_type=jnp.float32)
        return product.reshape(FRAMES, TOK_FRAME, HEADS, HEAD_DIM)
    queries = normed(project(0), query_gain).transpose(2, 0, 1, 3)
    key_rows = normed(project(1), key_gain).transpose(2, 0, 1, 3)
    values = project(2).astype(jnp.bfloat16).transpose(2, 0, 1, 3)

    def one_head(head_items):
        head_q, head_k, head_v, label, space_live, time_live = head_items
        return lax.cond(label == 1, time_head, space_head, head_q, head_k, head_v, space_live, time_live)
    mixed = lax.map(one_head, (queries, key_rows, values, labels, space_mask, time_mask))
    return mixed.transpose(1, 2, 0, 3).reshape(TOKENS, HEADS * HEAD_DIM).astype(jnp.bfloat16)
```

```python
import functools
import math

import jax
import jax.numpy as jnp
from jax import lax
from jax.experimental import pallas as pl
from jax.experimental.pallas import tpu as pltpu
from jax.sharding import PartitionSpec as P

STRIP = 8
BLOCK = 64
D = 3072
HD = 128
ROWS = 1024
FRAMES = 32
GROUPS = 8
QBLOCKS = 16
NEAR = 8
OUT = FRAMES // GROUPS
CHUNK = 768
PARTS = D // CHUNK
TILE = 256
EPSILON = 1e-06
SCALE = math.log2(math.e) / math.sqrt(HD)
BLOCKED = -16384.0
DEAD = 64
LABEL_ROWS = 16

bf16 = jnp.bfloat16
f32 = jnp.float32


def slots_of(labels):
    time = labels[1] + 2 * labels[2]
    return time, jnp.where(time == 0, 1, 0), jnp.where(time == 2, 1, 2)


def swapped(two_bits):
    return (two_bits & 1) * 2 + ((two_bits >> 1) & 1)


def owner_of(source, target, quarter):
    flip = (source >> 2) ^ (target >> 2)
    shift = (target - source) & 3
    return (quarter * 4 + swapped((shift - 2 * flip) & 3)) * 2 + flip


def handover():
    pairs = []
    for owner in range(FRAMES):
        flip = owner & 1
        shift = (swapped((owner >> 1) & 3) + 2 * flip) & 3
        for head in range(GROUPS):
            target = ((head >> 2) ^ flip) * 4 + ((head + shift) & 3)
            pairs.append((owner * GROUPS + head, owner * GROUPS + target))
    return pairs


def normed(x, gain):
    inverse = lax.rsqrt(jnp.mean(x * x, axis=-1, keepdims=True) + EPSILON)
    return (x * inverse * gain).astype(bf16)


def load_parts(tokens, weight, columns, tok, wts, sems):
    def copies(c):
        made = [
            pltpu.make_async_copy(
                tokens.at[:, pl.ds(c * CHUNK, CHUNK)], tok.at[:, pl.ds(c * CHUNK, CHUNK)], sems.at[c, 0]
            )
        ]
        for i, (k, slot) in enumerate(columns):
            made.append(
                pltpu.make_async_copy(
                    weight.at[k, pl.ds(c * CHUNK, CHUNK), pl.ds(pl.multiple_of(slot * HD, HD), HD)],
                    wts.at[pl.ds(c * CHUNK, CHUNK), pl.ds(i * HD, HD)],
                    sems.at[c, 1 + i],
                )
            )
        return made

    return copies


def project(tokens, weight, columns, tok, wts, acc, sems):
    copies = load_parts(tokens, weight, columns, tok, wts, sems)
    for c in range(2):
        for copy in copies(c):
            copy.start()
    for c in range(PARTS):
        for copy in copies(c):
            copy.wait()
        if c + 2 < PARTS:
            for copy in copies(c + 2):
                copy.start()
        for r in range(ROWS // TILE):
            rows = pl.ds(r * TILE, TILE)
            part = jnp.dot(
                tok[rows, pl.ds(c * CHUNK, CHUNK)], wts[pl.ds(c * CHUNK, CHUNK), :], preferred_element_type=f32
            )
            if c == 0:
                acc[rows, :] = part
            else:
                acc[rows, :] += part


def time_project(labels, tokens, weight, query_gain, key_gain, out, tok, wts, acc, sems):
    time, _, _ = slots_of(labels)
    project(tokens, weight, [(0, time), (1, time), (2, time)], tok, wts, acc, sems)
    head = lax.axis_index("head")
    for b in range(FRAMES):
        owner = owner_of(head, b // OUT, b % OUT)
        rows = pl.ds(b * FRAMES, FRAMES)
        out[owner, 0:FRAMES, :] = normed(acc[rows, 0:HD], query_gain[...] * SCALE)
        out[owner, FRAMES : 2 * FRAMES, :] = normed(acc[rows, HD : 2 * HD], key_gain[...])
        out[owner, 2 * FRAMES :, :] = acc[rows, 2 * HD :].astype(bf16)


def space_project(labels, live, tokens, weight, query_gain, key_gain, q, kv, up, down, lanes, tok, wts, acc, sems):
    _, first, second = slots_of(labels)
    columns = [(k, slot) for k in range(3) for slot in (first, second)]
    for h, slot in enumerate((first, second)):
        for side in range(2):
            base = (2 * h + side) * 32
            for j in range(32):
                lanes[base + j] = DEAD
            count = 0
            for b in range(QBLOCKS):
                column = 2 * QBLOCKS * side + b
                alive = live[slot, column]
                lanes[base + count] = jnp.where(alive > 0, column, DEAD)
                count = count + (alive > 0).astype(jnp.int32)
    project(tokens, weight, columns, tok, wts, acc, sems)
    for h in range(2):
        for r in range(ROWS // TILE):
            rows = pl.ds(r * TILE, TILE)
            q[h, rows, :] = normed(acc[rows, h * HD : (h + 1) * HD], query_gain[...] * SCALE)
            kv[h, 0, rows, :] = normed(acc[rows, (2 + h) * HD : (3 + h) * HD], key_gain[...])
            kv[h, 1, rows, :] = acc[rows, (4 + h) * HD : (5 + h) * HD].astype(bf16)
        for side, packed in enumerate((up, down)):
            for j in range(NEAR):
                block = lanes[(2 * h + side) * 32 + j] & (QBLOCKS - 1)
                rows = pl.ds(pl.multiple_of(block * BLOCK, BLOCK), BLOCK)
                for part in range(2):
                    packed[h, part, pl.ds(j * BLOCK, BLOCK), :] = kv[h, part, rows, :]


def one_hot(rows, lane):
    return (lax.broadcasted_iota(jnp.int32, (rows, HD), 1) == lane).astype(f32).astype(bf16)


def space_attend(labels, lanes, q, kv, below, above, mask, out, keys, vals, bias):
    time, first, second = slots_of(labels)
    h = pl.program_id(0)
    t = pl.program_id(1)
    near = NEAR * BLOCK

    @pl.when(t == 0)
    def _():
        slot = jnp.where(h == 0, first, second)
        frame = lax.axis_index("frame")
        table = mask[slot].astype(f32)
        lane = lax.broadcasted_iota(jnp.int32, (QBLOCKS, HD), 1)
        table = jnp.where((lane < QBLOCKS) & (frame == 0), 0.0, table)
        table = jnp.where((lane >= 2 * QBLOCKS) & (frame == FRAMES - 1), 0.0, table)
        bias[...] = (table - 1.0) * -BLOCKED
        keys[0:ROWS, 0:HD] = kv[0, 0]
        vals[0:ROWS, 0:HD] = kv[0, 1]
        for side, got in enumerate((below, above)):
            rows = pl.ds(ROWS + side * near, near)
            keys[rows, 0:HD] = got[0, 0]
            vals[rows, 0:HD] = got[0, 1]
            for j in range(NEAR):
                lane = lanes[(2 * h + side) * 32 + j]
                keys[pl.ds(ROWS + side * near + j * BLOCK, BLOCK), HD:] = one_hot(BLOCK, lane)
        for b in range(QBLOCKS):
            keys[pl.ds(b * BLOCK, BLOCK), HD:] = one_hot(BLOCK, QBLOCKS + b)
        vals[:, HD:] = jnp.ones((ROWS + 2 * near, HD), bf16)

    per = TILE // BLOCK
    rows = [
        jnp.broadcast_to(bias[pl.ds(t * per + i, 1), :], (BLOCK, HD)).astype(bf16) for i in range(per)
    ]
    query = jnp.concatenate([q[0], jnp.concatenate(rows, axis=0)], axis=1)
    total = jnp.zeros((TILE, 2 * HD), f32)
    width = 512
    for c in range((ROWS + 2 * near) // width):
        part = pl.ds(c * width, width)
        scores = lax.dot_general(query, keys[part, :], (((1,), (1,)), ((), ())), preferred_element_type=f32)
        weight = jnp.exp2(scores).astype(bf16)
        total = total + jnp.dot(weight, vals[part, :], preferred_element_type=f32)
    mixed = (total[:, 0:HD] / total[:, HD:]).astype(bf16)
    per_target = ROWS // GROUPS
    out[:, 0:per_target, :] = mixed.reshape(TILE // per_target, per_target, HD)
    out[:, per_target:, :] = jnp.full((TILE // per_target, LABEL_ROWS, HD), time.astype(f32)).astype(bf16)


def time_attend(labels, time_mask, got, out):
    time, _, _ = slots_of(labels)
    lane = lax.broadcasted_iota(jnp.int32, (16, HD), 1)
    row = lax.broadcasted_iota(jnp.int32, (16, HD), 0)
    same = (lane & 1) == (row >> 3)
    tables = []
    for a in range(4):
        allowed = jnp.zeros((16, HD), jnp.int32)
        for b in range(4):
            allowed = jnp.where((lane >> 1) == b, time_mask[time, a, b], allowed)
        table = jnp.where(same & (allowed == 1), 0.0, BLOCKED).astype(bf16)
        tables.append(jnp.broadcast_to(table[None], (8, 16, HD)))
    bias = jnp.concatenate(tables, axis=0).reshape(512, HD)
    key_frame = lax.broadcasted_iota(jnp.int32, (512, HD), 0)
    key_lane = lax.broadcasted_iota(jnp.int32, (512, HD), 1)
    mark = (((key_frame >> 7) * 2 + ((key_frame >> 3) & 1)) == key_lane).astype(f32).astype(bf16)
    ones = jnp.ones((512, HD), bf16)
    for u in range(2):
        def rows(part):
            return got[:, pl.ds(part * FRAMES + u * 16, 16), :].reshape(512, HD)

        query = jnp.concatenate([rows(0), bias], axis=1)
        keys = jnp.concatenate([rows(1), mark], axis=1)
        vals = jnp.concatenate([rows(2), ones], axis=1)
        scores = lax.dot_general(query, keys, (((1,), (1,)), ((), ())), preferred_element_type=f32)
        weight = jnp.exp2(scores).astype(bf16)
        total = jnp.dot(weight, vals, preferred_element_type=f32)
        mixed = (total[:, 0:HD] / total[:, HD:]).astype(bf16)
        out[:, pl.ds(u * 16, 16), :] = mixed.reshape(FRAMES, 16, HD)


def assemble(space, slot, timed, out):
    here = lax.axis_index("head")
    quarter = pl.program_id(0)
    for g in range(GROUPS):
        t = timed[owner_of(g, here, quarter)]
        place = slot[g, :, 0:HD]
        place = jnp.concatenate([place] * (FRAMES // LABEL_ROWS), axis=0)
        s0 = space[g, :, 0:HD]
        s1 = space[g, :, HD:]
        base = 3 * g * HD
        out[:, base : base + HD] = jnp.where(place == 0, t, s0)
        out[:, base + HD : base + 2 * HD] = jnp.where(place == 0, s0, jnp.where(place == 1, t, s1))
        out[:, base + 2 * HD : base + 3 * HD] = jnp.where(place == 2, t, s1)


def params(mib):
    return pltpu.CompilerParams(vmem_limit_bytes=mib * 2**20)


def cost(flops, moved, exps=0):
    return pl.CostEstimate(flops=int(flops), bytes_accessed=int(moved), transcendentals=int(exps))


SMEM = pl.BlockSpec(memory_space=pltpu.SMEM)
VMEM = pl.BlockSpec(memory_space=pltpu.VMEM)
ANY = pl.BlockSpec(memory_space=pl.ANY)


def on_device(tokens, qkv_weight, query_gain, key_gain, labels, space_mask, time_mask):
    gains = (query_gain.reshape(1, HD), key_gain.reshape(1, HD))
    sent = pl.pallas_call(
        time_project,
        out_shape=jax.ShapeDtypeStruct((FRAMES, 3 * FRAMES, HD), bf16),
        in_specs=[SMEM, ANY, ANY, VMEM, VMEM],
        out_specs=VMEM,
        scratch_shapes=[
            pltpu.VMEM((ROWS, D), bf16),
            pltpu.VMEM((D, 3 * HD), bf16),
            pltpu.VMEM((ROWS, 3 * HD), f32),
            pltpu.SemaphoreType.DMA((PARTS, 4)),
        ],
        compiler_params=params(28),
        cost_estimate=cost(2 * ROWS * D * 3 * HD, 9e6),
        name="time_project",
    )(labels, tokens, qkv_weight, *gains)
    got = lax.all_to_all(sent, "frame", split_axis=0, concat_axis=0, tiled=True)

    live = jnp.pad(jnp.max(space_mask, axis=1), ((0, 0), (0, HD - 3 * QBLOCKS)))
    pair = jax.ShapeDtypeStruct((2, 2, NEAR * BLOCK, HD), bf16)
    q, kv, up, down, lanes = pl.pallas_call(
        space_project,
        out_shape=(
            jax.ShapeDtypeStruct((2, ROWS, HD), bf16),
            jax.ShapeDtypeStruct((2, 2, ROWS, HD), bf16),
            pair,
            pair,
            jax.ShapeDtypeStruct((HD,), jnp.int32),
        ),
        in_specs=[SMEM, SMEM, ANY, ANY, VMEM, VMEM],
        out_specs=(VMEM, VMEM, VMEM, VMEM, SMEM),
        scratch_shapes=[
            pltpu.VMEM((ROWS, D), bf16),
            pltpu.VMEM((D, 6 * HD), bf16),
            pltpu.VMEM((ROWS, 6 * HD), f32),
            pltpu.SemaphoreType.DMA((PARTS, 7)),
        ],
        compiler_params=params(28),
        cost_estimate=cost(2 * ROWS * D * 6 * HD, 12e6),
        name="space_project",
    )(labels, live, tokens, qkv_weight, *gains)
    below = lax.ppermute(up, "frame", [(i, i + 1) for i in range(FRAMES - 1)])
    above = lax.ppermute(down, "frame", [(i + 1, i) for i in range(FRAMES - 1)])

    mask = jnp.pad(space_mask, ((0, 0), (0, 0), (0, HD - 3 * QBLOCKS)))
    total_keys = ROWS + 2 * NEAR * BLOCK
    per_target = ROWS // GROUPS
    near_spec = pl.BlockSpec((1, 2, NEAR * BLOCK, HD), lambda h, t: (h, 0, 0, 0))
    space_out = pl.pallas_call(
        space_attend,
        grid=(2, ROWS // TILE),
        out_shape=jax.ShapeDtypeStruct((GROUPS, per_target + LABEL_ROWS, 2 * HD), bf16),
        in_specs=[
            SMEM,
            SMEM,
            pl.BlockSpec((1, TILE, HD), lambda h, t: (h, t, 0)),
            pl.BlockSpec((1, 2, ROWS, HD), lambda h, t: (h, 0, 0, 0)),
            near_spec,
            near_spec,
            VMEM,
        ],
        out_specs=pl.BlockSpec((TILE // per_target, per_target + LABEL_ROWS, HD), lambda h, t: (t, 0, h)),
        scratch_shapes=[
            pltpu.VMEM((total_keys, 2 * HD), bf16),
            pltpu.VMEM((total_keys, 2 * HD), bf16),
            pltpu.VMEM((QBLOCKS, HD), f32),
        ],
        compiler_params=params(24),
        cost_estimate=cost(2 * 4 * ROWS * total_keys * 2 * HD, 4e6, 2 * ROWS * total_keys),
        name="space_attend",
    )(labels, lanes, q, kv, below, above, mask)
    space_all = lax.all_to_all(space_out, "head", split_axis=0, concat_axis=0, tiled=True)

    time_out = pl.pallas_call(
        time_attend,
        out_shape=jax.ShapeDtypeStruct((FRAMES, FRAMES, HD), bf16),
        in_specs=[SMEM, SMEM, VMEM],
        out_specs=VMEM,
        compiler_params=params(16),
        cost_estimate=cost(8 * 512 * 512 * 2 * HD, 1e6, 2 * 512 * 512),
        name="time_attend",
    )(labels, time_mask, got)
    moved = lax.ppermute(time_out, ("frame", "head"), handover())
    timed = lax.all_to_all(moved, "frame", split_axis=0, concat_axis=0, tiled=True)

    quarter = per_target // 4
    return pl.pallas_call(
        assemble,
        grid=(4,),
        out_shape=jax.ShapeDtypeStruct((per_target, 3 * GROUPS * HD), bf16),
        in_specs=[
            pl.BlockSpec((GROUPS, quarter, 2 * HD), lambda i: (0, i, 0)),
            pl.BlockSpec((GROUPS, LABEL_ROWS, 2 * HD), lambda i: (0, per_target // LABEL_ROWS, 0)),
            VMEM,
        ],
        out_specs=pl.BlockSpec((quarter, 3 * GROUPS * HD), lambda i: (i, 0)),
        compiler_params=params(16),
        cost_estimate=cost(1e6, 2e6),
        name="assemble",
    )(space_all, space_all, timed)


def solution(mesh):
    placed = (
        P("frame", None),
        P(None, None, "head"),
        P(),
        P(),
        P("head"),
        P("head", None, None),
        P("head", None, None),
    )
    return jax.shard_map(
        on_device, mesh=mesh, in_specs=placed, out_specs=P(("frame", "head"), None), check_vma=False
    )
```

```python
import math

import jax
import jax.numpy as jnp
from jax import lax
from jax.experimental import pallas as pl
from jax.experimental.pallas import tpu as pltpu
from jax.sharding import PartitionSpec as P

STRIP = 8
BLOCK = 64
D = 3072
HD = 128
ROWS = 1024
FRAMES = 32
GROUPS = 8
QBLOCKS = 16
NEAR = 8
CHUNK = 768
PARTS = D // CHUNK
TILE = 256
EPSILON = 1e-06
SCALE = math.log2(math.e) / math.sqrt(HD)
BLOCKED = -16384.0
DEAD = 64

bf16 = jnp.bfloat16
f32 = jnp.float32


def slots_of(labels):
    time = labels[1] + 2 * labels[2]
    return time, jnp.where(time == 0, 1, 0), jnp.where(time == 2, 1, 2)


def normed(x, gain):
    inverse = lax.rsqrt(jnp.mean(x * x, axis=-1, keepdims=True) + EPSILON)
    return (x * inverse * gain).astype(bf16)


def load_parts(tokens, weight, columns, tok, wts, sems):
    def copies(c):
        made = [
            pltpu.make_async_copy(
                tokens.at[:, pl.ds(c * CHUNK, CHUNK)], tok.at[:, pl.ds(c * CHUNK, CHUNK)], sems.at[c, 0]
            )
        ]
        for i, (k, slot) in enumerate(columns):
            made.append(
                pltpu.make_async_copy(
                    weight.at[k, pl.ds(c * CHUNK, CHUNK), pl.ds(pl.multiple_of(slot * HD, HD), HD)],
                    wts.at[pl.ds(c * CHUNK, CHUNK), pl.ds(i * HD, HD)],
                    sems.at[c, 1 + i],
                )
            )
        return made

    return copies


def project(tokens, weight, columns, tok, wts, acc, sems):
    copies = load_parts(tokens, weight, columns, tok, wts, sems)
    for c in range(2):
        for copy in copies(c):
            copy.start()
    for c in range(PARTS):
        for copy in copies(c):
            copy.wait()
        if c + 2 < PARTS:
            for copy in copies(c + 2):
                copy.start()
        part = jnp.dot(
            tok[:, pl.ds(c * CHUNK, CHUNK)], wts[pl.ds(c * CHUNK, CHUNK), :], preferred_element_type=f32
        )
        if c == 0:
            acc[...] = part
        else:
            acc[...] += part


def time_project(labels, tokens, weight, query_gain, key_gain, out, tok, wts, acc, sems):
    time, _, _ = slots_of(labels)
    project(tokens, weight, [(0, time), (1, time), (2, time)], tok, wts, acc, sems)
    for b in range(FRAMES):
        rows = pl.ds(b * FRAMES, FRAMES)
        out[b, 0:FRAMES, :] = normed(acc[rows, 0:HD], query_gain[...] * SCALE)
        out[b, FRAMES : 2 * FRAMES, :] = normed(acc[rows, HD : 2 * HD], key_gain[...])
        out[b, 2 * FRAMES :, :] = acc[rows, 2 * HD :].astype(bf16)


def space_project(labels, live, tokens, weight, query_gain, key_gain, q, kv, up, down, lanes, tok, wts, acc, sems):
    _, first, second = slots_of(labels)
    columns = [(k, slot) for k in range(3) for slot in (first, second)]
    for h, slot in enumerate((first, second)):
        for side in range(2):
            base = (2 * h + side) * 32
            for j in range(32):
                lanes[base + j] = DEAD
            count = 0
            for b in range(QBLOCKS):
                column = 2 * QBLOCKS * side + b
                alive = live[slot, column]
                lanes[base + count] = jnp.where(alive > 0, column, DEAD)
                count = count + (alive > 0).astype(jnp.int32)
    project(tokens, weight, columns, tok, wts, acc, sems)
    for h in range(2):
        for r in range(ROWS // TILE):
            rows = pl.ds(r * TILE, TILE)
            q[h, rows, :] = normed(acc[rows, h * HD : (h + 1) * HD], query_gain[...] * SCALE)
            kv[h, 0, rows, :] = normed(acc[rows, (2 + h) * HD : (3 + h) * HD], key_gain[...])
            kv[h, 1, rows, :] = acc[rows, (4 + h) * HD : (5 + h) * HD].astype(bf16)
        for side, packed in enumerate((up, down)):
            for j in range(NEAR):
                block = lanes[(2 * h + side) * 32 + j] & (QBLOCKS - 1)
                rows = pl.ds(pl.multiple_of(block * BLOCK, BLOCK), BLOCK)
                for part in range(2):
                    packed[h, part, pl.ds(j * BLOCK, BLOCK), :] = kv[h, part, rows, :]


def one_hot(rows, lane):
    return (lax.broadcasted_iota(jnp.int32, (rows, HD), 1) == lane).astype(f32).astype(bf16)


def space_attend(labels, lanes, q, kv, below, above, mask, after, out, keys, vals):
    _, *slots = slots_of(labels)
    frame = lax.axis_index("frame")
    near = NEAR * BLOCK
    for b in range(QBLOCKS):
        own = one_hot(BLOCK, QBLOCKS + b)
        for h in range(2):
            keys[h, pl.ds(b * BLOCK, BLOCK), HD:] = own
    for h in range(2):
        keys[h, 0:ROWS, 0:HD] = kv[h, 0]
        vals[h, 0:ROWS, 0:HD] = kv[h, 1]
        vals[h, :, HD:] = jnp.ones((ROWS + 2 * near, HD), bf16)
        for side, got in enumerate((below, above)):
            rows = pl.ds(ROWS + side * near, near)
            keys[h, rows, 0:HD] = got[h, 0]
            vals[h, rows, 0:HD] = got[h, 1]
            for j in range(NEAR):
                lane = lanes[(2 * h + side) * 32 + j]
                keys[h, pl.ds(ROWS + side * near + j * BLOCK, BLOCK), HD:] = one_hot(BLOCK, lane)

    lane = lax.broadcasted_iota(jnp.int32, (QBLOCKS, HD), 1)
    per = TILE // BLOCK
    width = 512
    per_target = ROWS // GROUPS
    for h in range(2):
        table = mask[slots[h]].astype(f32)
        table = jnp.where((lane < QBLOCKS) & (frame == 0), 0.0, table)
        table = jnp.where((lane >= 2 * QBLOCKS) & (frame == FRAMES - 1), 0.0, table)
        bias = (table - 1.0) * -BLOCKED
        for t in range(ROWS // TILE):
            rows = [jnp.broadcast_to(bias[t * per + i : t * per + i + 1], (BLOCK, HD)) for i in range(per)]
            query = jnp.concatenate(
                [q[h, pl.ds(t * TILE, TILE), :], jnp.concatenate(rows, axis=0).astype(bf16)], axis=1
            )
            total = jnp.zeros((TILE, 2 * HD), f32)
            for c in range((ROWS + 2 * near) // width):
                part = pl.ds(c * width, width)
                scores = lax.dot_general(
                    query, keys[h, part, :], (((1,), (1,)), ((), ())), preferred_element_type=f32
                )
                weight = jnp.exp2(scores).astype(bf16)
                total = total + jnp.dot(weight, vals[h, part, :], preferred_element_type=f32)
            mixed = (total[:, 0:HD] / total[:, HD:]).astype(bf16)
            targets = pl.ds(t * TILE // per_target, TILE // per_target)
            column = pl.ds(pl.multiple_of(slots[h] * HD, HD), HD)
            out[targets, :, column] = mixed.reshape(-1, per_target, HD)


def time_attend(labels, time_mask, got, out, done):
    done[...] = jnp.zeros_like(done)
    time, _, _ = slots_of(labels)
    lane = lax.broadcasted_iota(jnp.int32, (16, HD), 1)
    row = lax.broadcasted_iota(jnp.int32, (16, HD), 0)
    same = (lane & 1) == (row >> 3)
    tables = []
    for a in range(4):
        allowed = jnp.zeros((16, HD), jnp.int32)
        for b in range(4):
            allowed = jnp.where((lane >> 1) == b, time_mask[time, a, b], allowed)
        table = jnp.where(same & (allowed == 1), 0.0, BLOCKED).astype(bf16)
        tables.append(jnp.broadcast_to(table[None], (8, 16, HD)))
    bias = jnp.concatenate(tables, axis=0).reshape(512, HD)
    key_frame = lax.broadcasted_iota(jnp.int32, (512, HD), 0)
    key_lane = lax.broadcasted_iota(jnp.int32, (512, HD), 1)
    mark = (((key_frame >> 7) * 2 + ((key_frame >> 3) & 1)) == key_lane).astype(f32).astype(bf16)
    ones = jnp.ones((512, HD), bf16)
    for u in range(2):
        def rows(part):
            return got[:, pl.ds(part * FRAMES + u * 16, 16), :].reshape(512, HD)

        query = jnp.concatenate([rows(0), bias], axis=1)
        keys = jnp.concatenate([rows(1), mark], axis=1)
        vals = jnp.concatenate([rows(2), ones], axis=1)
        scores = lax.dot_general(query, keys, (((1,), (1,)), ((), ())), preferred_element_type=f32)
        weight = jnp.exp2(scores).astype(bf16)
        total = jnp.dot(weight, vals, preferred_element_type=f32)
        mixed = (total[:, 0:HD] / total[:, HD:]).astype(bf16)
        out[:, pl.ds(u * 16, 16), :] = mixed.reshape(FRAMES, 16, HD)


def merge(labels, space, timed, out, sem):
    time, _, _ = slots_of(labels)
    column = pl.ds(pl.multiple_of(time * HD, HD), HD)
    copy = pltpu.make_async_copy(timed, out.at[:, :, column], sem)
    copy.start()
    copy.wait()


def assemble(parts, out, sems):
    width = parts.shape[2]
    copies = [
        pltpu.make_async_copy(parts.at[g], out.at[:, pl.ds(g * width, width)], sems.at[g]) for g in range(GROUPS)
    ]
    for copy in copies:
        copy.start()
    for copy in copies:
        copy.wait()


def params(mib):
    return pltpu.CompilerParams(vmem_limit_bytes=mib * 2**20)


def cost(flops, moved, exps=0):
    return pl.CostEstimate(flops=int(flops), bytes_accessed=int(moved), transcendentals=int(exps))


SMEM = pl.BlockSpec(memory_space=pltpu.SMEM)
VMEM = pl.BlockSpec(memory_space=pltpu.VMEM)
ANY = pl.BlockSpec(memory_space=pl.ANY)


def on_device(tokens, qkv_weight, query_gain, key_gain, labels, space_mask, time_mask):
    gains = (query_gain.reshape(1, HD), key_gain.reshape(1, HD))
    sent = pl.pallas_call(
        time_project,
        out_shape=jax.ShapeDtypeStruct((FRAMES, 3 * FRAMES, HD), bf16),
        in_specs=[SMEM, ANY, ANY, VMEM, VMEM],
        out_specs=VMEM,
        scratch_shapes=[
            pltpu.VMEM((ROWS, D), bf16),
            pltpu.VMEM((D, 3 * HD), bf16),
            pltpu.VMEM((ROWS, 3 * HD), f32),
            pltpu.SemaphoreType.DMA((PARTS, 4)),
        ],
        compiler_params=params(60),
        cost_estimate=cost(2 * ROWS * D * 3 * HD, 9e6),
        name="time_project",
    )(labels, tokens, qkv_weight, *gains)
    got = lax.all_to_all(sent, "frame", split_axis=0, concat_axis=0, tiled=True)

    live = jnp.pad(jnp.max(space_mask, axis=1), ((0, 0), (0, HD - 3 * QBLOCKS)))
    pair = jax.ShapeDtypeStruct((2, 2, NEAR * BLOCK, HD), bf16)
    q, kv, up, down, lanes = pl.pallas_call(
        space_project,
        out_shape=(
            jax.ShapeDtypeStruct((2, ROWS, HD), bf16),
            jax.ShapeDtypeStruct((2, 2, ROWS, HD), bf16),
            pair,
            pair,
            jax.ShapeDtypeStruct((HD,), jnp.int32),
        ),
        in_specs=[SMEM, SMEM, ANY, ANY, VMEM, VMEM],
        out_specs=(VMEM, VMEM, VMEM, VMEM, SMEM),
        scratch_shapes=[
            pltpu.VMEM((ROWS, D), bf16),
            pltpu.VMEM((D, 6 * HD), bf16),
            pltpu.VMEM((ROWS, 6 * HD), f32),
            pltpu.SemaphoreType.DMA((PARTS, 7)),
        ],
        compiler_params=params(58),
        cost_estimate=cost(2 * ROWS * D * 6 * HD, 12e6),
        name="space_project",
    )(labels, live, tokens, qkv_weight, *gains)
    below = lax.ppermute(up, "frame", [(i, i + 1) for i in range(FRAMES - 1)])
    above = lax.ppermute(down, "frame", [(i + 1, i) for i in range(FRAMES - 1)])

    time_out, done = pl.pallas_call(
        time_attend,
        out_shape=(jax.ShapeDtypeStruct((FRAMES, FRAMES, HD), bf16), jax.ShapeDtypeStruct((8, HD), f32)),
        in_specs=[SMEM, SMEM, VMEM],
        out_specs=(VMEM, VMEM),
        compiler_params=params(16),
        cost_estimate=cost(8 * 512 * 512 * 2 * HD, 1e6, 2 * 512 * 512),
        name="time_attend",
    )(labels, time_mask, got)

    mask = jnp.pad(space_mask, ((0, 0), (0, 0), (0, HD - 3 * QBLOCKS)))
    total_keys = ROWS + 2 * NEAR * BLOCK
    per_target = ROWS // GROUPS
    space_out = pl.pallas_call(
        space_attend,
        out_shape=jax.ShapeDtypeStruct((GROUPS, per_target, 3 * HD), bf16),
        in_specs=[SMEM, SMEM] + [VMEM] * 5 + [ANY],
        out_specs=VMEM,
        scratch_shapes=[
            pltpu.VMEM((2, total_keys, 2 * HD), bf16),
            pltpu.VMEM((2, total_keys, 2 * HD), bf16),
        ],
        compiler_params=params(16),
        cost_estimate=cost(2 * 4 * ROWS * total_keys * 2 * HD, 4e6, 2 * ROWS * total_keys),
        name="space_attend",
    )(labels, lanes, q, kv, below, above, mask, done)
    timed = lax.all_to_all(time_out, "frame", split_axis=0, concat_axis=0, tiled=True)
    merged = pl.pallas_call(
        merge,
        out_shape=jax.ShapeDtypeStruct((GROUPS, per_target, 3 * HD), bf16),
        in_specs=[SMEM, ANY, ANY],
        out_specs=ANY,
        scratch_shapes=[pltpu.SemaphoreType.DMA],
        input_output_aliases={1: 0},
        compiler_params=params(16),
        cost_estimate=cost(1, 5e5),
        name="merge",
    )(labels, space_out, timed.reshape(GROUPS, per_target, HD))
    parts = lax.all_to_all(merged, "head", split_axis=0, concat_axis=0, tiled=True)
    return pl.pallas_call(
        assemble,
        out_shape=jax.ShapeDtypeStruct((per_target, 3 * GROUPS * HD), bf16),
        in_specs=[ANY],
        out_specs=ANY,
        scratch_shapes=[pltpu.SemaphoreType.DMA((GROUPS,))],
        compiler_params=params(16),
        cost_estimate=cost(1, 2e6),
        name="assemble",
    )(parts)


def solution(mesh):
    placed = (
        P("frame", None),
        P(None, None, "head"),
        P(),
        P(),
        P("head"),
        P("head", None, None),
        P("head", None, None),
    )
    return jax.shard_map(
        on_device, mesh=mesh, in_specs=placed, out_specs=P(("frame", "head"), None), check_vma=False
    )
```

```python
import math

import jax
import jax.numpy as jnp
from jax import lax
from jax.experimental import pallas as pl
from jax.experimental.pallas import tpu as pltpu
from jax.sharding import PartitionSpec as P

STRIP = 8
BLOCK = 64
D = 3072
HD = 128
ROWS = 1024
FRAMES = 32
GROUPS = 8
QBLOCKS = 16
NEAR = 8
CHUNK = 768
PARTS = D // CHUNK
TILE = 256
EPSILON = 1e-06
SCALE = math.log2(math.e) / math.sqrt(HD)
OUT = FRAMES // GROUPS
LABEL_ROWS = 16
BLOCKED = -16384.0
DEAD = 64

SPACE_MIB = 58

bf16 = jnp.bfloat16
f32 = jnp.float32


def slots_of(labels):
    time = labels[1] + 2 * labels[2]
    return time, jnp.where(time == 0, 1, 0), jnp.where(time == 2, 1, 2)


def swapped(two_bits):
    return (two_bits & 1) * 2 + ((two_bits >> 1) & 1)


def owner_of(source, target, quarter):
    flip = (source >> 2) ^ (target >> 2)
    shift = (target - source) & 3
    return (quarter * 4 + swapped((shift - 2 * flip) & 3)) * 2 + flip


def handover():
    pairs = []
    for owner in range(FRAMES):
        flip = owner & 1
        shift = (swapped((owner >> 1) & 3) + 2 * flip) & 3
        for head in range(GROUPS):
            target = ((head >> 2) ^ flip) * 4 + ((head + shift) & 3)
            pairs.append((owner * GROUPS + head, owner * GROUPS + target))
    return pairs


def target_of(head, step):
    return ((head >> 2) ^ (step >> 2)) * 4 + ((head + step) & 3)


def source_of(head, step):
    return ((head >> 2) ^ (step >> 2)) * 4 + ((head - step) & 3)


def normed(x, gain):
    inverse = lax.rsqrt(jnp.mean(x * x, axis=-1, keepdims=True) + EPSILON)
    return (x * inverse * gain).astype(bf16)


def load_parts(tokens, weight, columns, tok, wts, sems):
    def copies(c):
        made = [
            pltpu.make_async_copy(
                tokens.at[:, pl.ds(c * CHUNK, CHUNK)], tok.at[:, pl.ds(c * CHUNK, CHUNK)], sems.at[c, 0]
            )
        ]
        for i, (k, slot) in enumerate(columns):
            made.append(
                pltpu.make_async_copy(
                    weight.at[k, pl.ds(c * CHUNK, CHUNK), pl.ds(pl.multiple_of(slot * HD, HD), HD)],
                    wts.at[pl.ds(c * CHUNK, CHUNK), pl.ds(i * HD, HD)],
                    sems.at[c, 1 + i],
                )
            )
        return made

    return copies


def project(tokens, weight, columns, tok, wts, acc, sems, meanwhile=None):
    copies = load_parts(tokens, weight, columns, tok, wts, sems)
    for c in range(2):
        for copy in copies(c):
            copy.start()
    if meanwhile is not None:
        meanwhile()
    for c in range(PARTS):
        for copy in copies(c):
            copy.wait()
        if c + 2 < PARTS:
            for copy in copies(c + 2):
                copy.start()
        part = jnp.dot(
            tok[:, pl.ds(c * CHUNK, CHUNK)], wts[pl.ds(c * CHUNK, CHUNK), :], preferred_element_type=f32
        )
        if c == 0:
            acc[...] = part
        else:
            acc[...] += part


def time_project(labels, tokens, weight, query_gain, key_gain, out, tok, wts, acc, sems):
    time, _, _ = slots_of(labels)
    project(tokens, weight, [(0, time), (1, time), (2, time)], tok, wts, acc, sems)
    head = lax.axis_index("head")
    for b in range(FRAMES):
        owner = owner_of(head, b // OUT, b % OUT)
        rows = pl.ds(b * FRAMES, FRAMES)
        out[owner, 0:FRAMES, :] = normed(acc[rows, 0:HD], query_gain[...] * SCALE)
        out[owner, FRAMES : 2 * FRAMES, :] = normed(acc[rows, HD : 2 * HD], key_gain[...])
        out[owner, 2 * FRAMES :, :] = acc[rows, 2 * HD :].astype(bf16)


def list_near(labels, live, lanes):
    _, *slots = slots_of(labels)
    for h in range(2):
        for side in range(2):
            base = (2 * h + side) * 32
            for j in range(NEAR):
                lanes[base + j] = DEAD
            count = 0
            for b in range(QBLOCKS):
                column = 2 * QBLOCKS * side + b
                alive = live[slots[h], column] > 0
                lanes[base + count] = jnp.where(alive, column, DEAD)
                count = count + alive.astype(jnp.int32)


def space_project(labels, live, tokens, weight, query_gain, key_gain, q, kv, up, down, tok, wts, acc, lanes, sems):
    _, first, second = slots_of(labels)
    columns = [(k, slot) for k in range(3) for slot in (first, second)]
    project(tokens, weight, columns, tok, wts, acc, sems, lambda: list_near(labels, live, lanes))
    for h in range(2):
        for r in range(ROWS // TILE):
            rows = pl.ds(r * TILE, TILE)
            q[h, rows, :] = normed(acc[rows, h * HD : (h + 1) * HD], query_gain[...] * SCALE)
            kv[h, 0, rows, :] = normed(acc[rows, (2 + h) * HD : (3 + h) * HD], key_gain[...])
            kv[h, 1, rows, :] = acc[rows, (4 + h) * HD : (5 + h) * HD].astype(bf16)
        for side, packed in enumerate((up, down)):
            for j in range(NEAR):
                block = lanes[(2 * h + side) * 32 + j] & (QBLOCKS - 1)
                rows = pl.ds(pl.multiple_of(block * BLOCK, BLOCK), BLOCK)
                for part in range(2):
                    packed[h, part, pl.ds(j * BLOCK, BLOCK), :] = kv[h, part, rows, :]


def one_hot(rows, lane):
    return (lax.broadcasted_iota(jnp.int32, (rows, HD), 1) == lane).astype(f32).astype(bf16)


def space_attend(labels, live, mask, q, kv, below, above, after, *rest):
    outs = rest[:GROUPS]
    keys, vals, query, bias, lanes, sems = rest[GROUPS:]
    time, *slots = slots_of(labels)
    frame = lax.axis_index("frame")
    head = lax.axis_index("head")
    near = NEAR * BLOCK
    rows = [pl.ds(0, ROWS), pl.ds(ROWS, near), pl.ds(ROWS + near, near)]
    left = pl.ds(0, HD)

    def copies(h):
        made = [pltpu.make_async_copy(q.at[h], query.at[h, :, left], sems.at[h, 0])]
        for i, got in enumerate((kv, below, above)):
            for part, kept in enumerate((keys, vals)):
                made.append(
                    pltpu.make_async_copy(got.at[h, part], kept.at[h, rows[i], left], sems.at[h, 1 + 2 * i + part])
                )
        return made

    for h in range(2):
        for copy in copies(h):
            copy.start()
    list_near(labels, live, lanes)
    lane = lax.broadcasted_iota(jnp.int32, (QBLOCKS, HD), 1)
    for h in range(2):
        table = mask[slots[h]].astype(f32)
        table = jnp.where((lane < QBLOCKS) & (frame == 0), 0.0, table)
        table = jnp.where((lane >= 2 * QBLOCKS) & (frame == FRAMES - 1), 0.0, table)
        bias[...] = (table - 1.0) * -BLOCKED
        for a in range(QBLOCKS):
            wide = jnp.broadcast_to(bias[a : a + 1, :], (BLOCK, HD)).astype(bf16)
            query[h, pl.ds(a * BLOCK, BLOCK), HD:] = wide
        vals[h, :, HD:] = jnp.ones((ROWS + 2 * near, HD), bf16)
        for b in range(QBLOCKS):
            keys[h, pl.ds(b * BLOCK, BLOCK), HD:] = one_hot(BLOCK, QBLOCKS + b)
        for side in range(2):
            for j in range(NEAR):
                mark = one_hot(BLOCK, lanes[(2 * h + side) * 32 + j])
                keys[h, pl.ds(ROWS + side * near + j * BLOCK, BLOCK), HD:] = mark

    per_target = ROWS // GROUPS
    width = 512
    for h in range(2):
        for copy in copies(h):
            copy.wait()
        for step in range(0, GROUPS, 2):
            tiles = []
            for s in (step, step + 1):
                start = pl.multiple_of(target_of(head, s) * per_target, per_target)
                tiles.append(query[h, pl.ds(start, per_target), :])
            tile = jnp.concatenate(tiles, axis=0)
            total = jnp.zeros((2 * per_target, 2 * HD), f32)
            for c in range((ROWS + 2 * near) // width):
                part = pl.ds(c * width, width)
                scores = lax.dot_general(
                    tile, keys[h, part, :], (((1,), (1,)), ((), ())), preferred_element_type=f32
                )
                weight = jnp.exp2(scores).astype(bf16)
                total = total + jnp.dot(weight, vals[h, part, :], preferred_element_type=f32)
            mixed = (total[:, 0:HD] / total[:, HD:]).astype(bf16)
            for i in range(2):
                done = mixed[i * per_target : (i + 1) * per_target]
                outs[step + i][0:per_target, h * HD : (h + 1) * HD] = done
    label = jnp.full((LABEL_ROWS, 2 * HD), time.astype(f32)).astype(bf16)
    for out in outs:
        out[per_target:, :] = label


def time_attend(labels, time_mask, got, out, done):
    done[...] = jnp.zeros_like(done)
    time, _, _ = slots_of(labels)
    lane = lax.broadcasted_iota(jnp.int32, (16, HD), 1)
    row = lax.broadcasted_iota(jnp.int32, (16, HD), 0)
    same = (lane & 1) == (row >> 3)
    tables = []
    for a in range(4):
        allowed = jnp.zeros((16, HD), jnp.int32)
        for b in range(4):
            allowed = jnp.where((lane >> 1) == b, time_mask[time, a, b], allowed)
        table = jnp.where(same & (allowed == 1), 0.0, BLOCKED).astype(bf16)
        tables.append(jnp.broadcast_to(table[None], (8, 16, HD)))
    bias = jnp.concatenate(tables, axis=0).reshape(512, HD)
    key_frame = lax.broadcasted_iota(jnp.int32, (512, HD), 0)
    key_lane = lax.broadcasted_iota(jnp.int32, (512, HD), 1)
    mark = (((key_frame >> 7) * 2 + ((key_frame >> 3) & 1)) == key_lane).astype(f32).astype(bf16)
    ones = jnp.ones((512, HD), bf16)
    for u in range(2):
        def rows(part):
            return got[:, pl.ds(part * FRAMES + u * 16, 16), :].reshape(512, HD)

        query = jnp.concatenate([rows(0), bias], axis=1)
        keys = jnp.concatenate([rows(1), mark], axis=1)
        vals = jnp.concatenate([rows(2), ones], axis=1)
        scores = lax.dot_general(query, keys, (((1,), (1,)), ((), ())), preferred_element_type=f32)
        weight = jnp.exp2(scores).astype(bf16)
        total = jnp.dot(weight, vals, preferred_element_type=f32)
        mixed = (total[:, 0:HD] / total[:, HD:]).astype(bf16)
        out[:, pl.ds(u * 16, 16), :] = mixed.reshape(FRAMES, 16, HD)


def assemble(timed, *rest):
    parts, out = rest[:GROUPS], rest[GROUPS]
    here = lax.axis_index("head")
    per_target = ROWS // GROUPS
    quarter = per_target // OUT
    for step in range(GROUPS):
        group = source_of(here, step)
        part = parts[step]
        label = jnp.concatenate([part[per_target:, 0:HD]] * (quarter // LABEL_ROWS), axis=0)
        for i in range(OUT):
            rows = pl.ds(i * quarter, quarter)
            t = timed[owner_of(group, here, i)]
            s0 = part[rows, 0:HD]
            s1 = part[rows, HD:]
            heads = (
                jnp.where(label == 0, t, s0),
                jnp.where(label == 0, s0, jnp.where(label == 1, t, s1)),
                jnp.where(label == 2, t, s1),
            )
            for j, values in enumerate(heads):
                out[rows, pl.ds(pl.multiple_of((3 * group + j) * HD, HD), HD)] = values


def params(mib):
    return pltpu.CompilerParams(vmem_limit_bytes=mib * 2**20)


def cost(flops, moved, exps=0):
    return pl.CostEstimate(flops=int(flops), bytes_accessed=int(moved), transcendentals=int(exps))


SMEM = pl.BlockSpec(memory_space=pltpu.SMEM)
VMEM = pl.BlockSpec(memory_space=pltpu.VMEM)
ANY = pl.BlockSpec(memory_space=pl.ANY)


def on_device(tokens, qkv_weight, query_gain, key_gain, labels, space_mask, time_mask):
    gains = (query_gain.reshape(1, HD), key_gain.reshape(1, HD))
    sent = pl.pallas_call(
        time_project,
        out_shape=jax.ShapeDtypeStruct((FRAMES, 3 * FRAMES, HD), bf16),
        in_specs=[SMEM, ANY, ANY, VMEM, VMEM],
        out_specs=VMEM,
        scratch_shapes=[
            pltpu.VMEM((ROWS, D), bf16),
            pltpu.VMEM((D, 3 * HD), bf16),
            pltpu.VMEM((ROWS, 3 * HD), f32),
            pltpu.SemaphoreType.DMA((PARTS, 4)),
        ],
        compiler_params=params(60),
        cost_estimate=cost(2 * ROWS * D * 3 * HD, 9e6),
        name="time_project",
    )(labels, tokens, qkv_weight, *gains)
    got = lax.all_to_all(sent, "frame", split_axis=0, concat_axis=0, tiled=True)

    live = jnp.pad(jnp.max(space_mask, axis=1), ((0, 0), (0, HD - 3 * QBLOCKS)))
    pair = jax.ShapeDtypeStruct((2, 2, NEAR * BLOCK, HD), bf16)
    q, kv, up, down = pl.pallas_call(
        space_project,
        out_shape=(
            jax.ShapeDtypeStruct((2, ROWS, HD), bf16),
            jax.ShapeDtypeStruct((2, 2, ROWS, HD), bf16),
            pair,
            pair,
        ),
        in_specs=[SMEM, SMEM, ANY, ANY, VMEM, VMEM],
        out_specs=(VMEM, VMEM, VMEM, VMEM),
        scratch_shapes=[
            pltpu.VMEM((ROWS, D), bf16),
            pltpu.VMEM((D, 6 * HD), bf16),
            pltpu.VMEM((ROWS, 6 * HD), f32),
            pltpu.SMEM((HD,), jnp.int32),
            pltpu.SemaphoreType.DMA((PARTS, 7)),
        ],
        compiler_params=params(58),
        cost_estimate=cost(2 * ROWS * D * 6 * HD, 12e6),
        name="space_project",
    )(labels, live, tokens, qkv_weight, *gains)
    below = lax.ppermute(up, "frame", [(i, i + 1) for i in range(FRAMES - 1)])
    above = lax.ppermute(down, "frame", [(i + 1, i) for i in range(FRAMES - 1)])

    time_out, done = pl.pallas_call(
        time_attend,
        out_shape=(jax.ShapeDtypeStruct((FRAMES, FRAMES, HD), bf16), jax.ShapeDtypeStruct((8, HD), f32)),
        in_specs=[SMEM, SMEM, VMEM],
        out_specs=(VMEM, VMEM),
        compiler_params=params(16),
        cost_estimate=cost(8 * 512 * 512 * 2 * HD, 1e6, 2 * 512 * 512),
        name="time_attend",
    )(labels, time_mask, got)

    mask = jnp.pad(space_mask, ((0, 0), (0, 0), (0, HD - 3 * QBLOCKS)))
    total_keys = ROWS + 2 * NEAR * BLOCK
    per_target = ROWS // GROUPS
    space_outs = pl.pallas_call(
        space_attend,
        out_shape=[jax.ShapeDtypeStruct((per_target + LABEL_ROWS, 2 * HD), bf16)] * GROUPS,
        in_specs=[SMEM, SMEM, VMEM] + [ANY] * 5,
        out_specs=[VMEM] * GROUPS,
        scratch_shapes=[
            pltpu.VMEM((2, total_keys, 2 * HD), bf16),
            pltpu.VMEM((2, total_keys, 2 * HD), bf16),
            pltpu.VMEM((2, ROWS, 2 * HD), bf16),
            pltpu.VMEM((QBLOCKS, HD), f32),
            pltpu.SMEM((HD,), jnp.int32),
            pltpu.SemaphoreType.DMA((2, 7)),
        ],
        compiler_params=params(SPACE_MIB),
        cost_estimate=cost(2 * 4 * ROWS * total_keys * 2 * HD, 4e6, 2 * ROWS * total_keys),
        name="space_attend",
    )(labels, live, mask, q, kv, below, above, done)
    moved = lax.ppermute(time_out, ("frame", "head"), handover())
    moved, *space_outs = lax.optimization_barrier((moved, *space_outs))
    timed = lax.all_to_all(moved, "frame", split_axis=0, concat_axis=0, tiled=True)
    parts = [space_outs[0]]
    for step in range(1, GROUPS):
        steps = [(h, int(target_of(h, step))) for h in range(GROUPS)]
        parts.append(lax.ppermute(space_outs[step], "head", steps))
    return pl.pallas_call(
        assemble,
        out_shape=jax.ShapeDtypeStruct((per_target, 3 * GROUPS * HD), bf16),
        in_specs=[VMEM] * (1 + GROUPS),
        out_specs=VMEM,
        compiler_params=params(16),
        cost_estimate=cost(1e6, 2e6),
        name="assemble",
    )(timed, *parts)


def solution(mesh):
    placed = (
        P("frame", None),
        P(None, None, "head"),
        P(),
        P(),
        P("head"),
        P("head", None, None),
        P("head", None, None),
    )
    return jax.shard_map(
        on_device, mesh=mesh, in_specs=placed, out_specs=P(("frame", "head"), None), check_vma=False
    )
```

```python
import math

import jax
import jax.numpy as jnp
from jax import lax
from jax.experimental import pallas as pl
from jax.experimental.pallas import tpu as pltpu
from jax.sharding import PartitionSpec as P

STRIP = 8
BLOCK = 64
D = 3072
HD = 128
ROWS = 1024
FRAMES = 32
GROUPS = 8
QBLOCKS = 16
NEAR = 8
CHUNKS = (512, 768, 768, 768, 256)
STARTS = tuple(sum(CHUNKS[:c]) for c in range(len(CHUNKS)))
PARTS = len(CHUNKS)
TILE = 256
EPSILON = 1e-06
SCALE = math.log2(math.e) / math.sqrt(HD)
BLOCKED = -16384.0
DEAD = 64

bf16 = jnp.bfloat16
f32 = jnp.float32


def slots_of(labels):
    time = labels[1] + 2 * labels[2]
    return time, jnp.where(time == 0, 1, 0), jnp.where(time == 2, 1, 2)


def normed(x, gain):
    inverse = lax.rsqrt(jnp.mean(x * x, axis=-1, keepdims=True) + EPSILON)
    return (x * inverse * gain).astype(bf16)


def project(tokens, weight, columns, tok, wts, acc, sems, meanwhile=None):
    def copies(c):
        part = pl.ds(STARTS[c], CHUNKS[c])
        made = [pltpu.make_async_copy(tokens.at[:, part], tok.at[:, part], sems.at[c, 0])]
        for i, (k, slot) in enumerate(columns):
            column = pl.ds(pl.multiple_of(slot * HD, HD), HD)
            made.append(
                pltpu.make_async_copy(weight.at[k, part, column], wts.at[part, pl.ds(i * HD, HD)], sems.at[c, 1 + i])
            )
        return made

    for c in range(2):
        for copy in copies(c):
            copy.start()
    if meanwhile is not None:
        meanwhile()
    for c in range(PARTS):
        for copy in copies(c):
            copy.wait()
        if c + 2 < PARTS:
            for copy in copies(c + 2):
                copy.start()
        part = pl.ds(STARTS[c], CHUNKS[c])
        product = jnp.dot(tok[:, part], wts[part, :], preferred_element_type=f32)
        if c == 0:
            acc[...] = product
        else:
            acc[...] += product


def time_project(labels, tokens, weight, query_gain, key_gain, out, made, tok, wts, acc, sems, out_sems):
    time, _, _ = slots_of(labels)
    project(tokens, weight, [(0, time), (1, time), (2, time)], tok, wts, acc, sems)
    copies = []
    for b in range(FRAMES):
        rows = pl.ds(b * FRAMES, FRAMES)
        made[b, 0:FRAMES, :] = normed(acc[rows, 0:HD], query_gain[...] * SCALE)
        made[b, FRAMES : 2 * FRAMES, :] = normed(acc[rows, HD : 2 * HD], key_gain[...])
        made[b, 2 * FRAMES :, :] = acc[rows, 2 * HD :].astype(bf16)
        if b % 8 == 7:
            group = pl.ds(b - 7, 8)
            copies.append(pltpu.make_async_copy(made.at[group], out.at[group], out_sems.at[b // 8]))
            copies[-1].start()
    for copy in copies:
        copy.wait()


def list_near(labels, live, lanes):
    _, *slots = slots_of(labels)
    for h in range(2):
        for side in range(2):
            base = (2 * h + side) * 32
            for j in range(32):
                lanes[base + j] = DEAD
            count = 0
            for b in range(QBLOCKS):
                column = 2 * QBLOCKS * side + b
                alive = live[slots[h], column] > 0
                lanes[base + count] = jnp.where(alive, column, DEAD)
                count = count + alive.astype(jnp.int32)


def space_project(labels, live, tokens, weight, query_gain, key_gain, *rest):
    q_out, kv_out, up_out, down_out, lanes, q, kv, up, down, tok, wts, acc, sems, out_sems = rest
    _, first, second = slots_of(labels)
    columns = [(k, slot) for k in range(3) for slot in (first, second)]
    project(tokens, weight, columns, tok, wts, acc, sems, lambda: list_near(labels, live, lanes))
    copies = []

    def send(source, target):
        copies.append(pltpu.make_async_copy(source, target, out_sems.at[len(copies)]))
        copies[-1].start()

    for r in range(ROWS // TILE):
        rows = pl.ds(r * TILE, TILE)
        for h in range(2):
            kv[h, 0, rows, :] = normed(acc[rows, (2 + h) * HD : (3 + h) * HD], key_gain[...])
            kv[h, 1, rows, :] = acc[rows, (4 + h) * HD : (5 + h) * HD].astype(bf16)
        send(kv.at[:, :, rows], kv_out.at[:, :, rows])
    for side, (packed, target) in enumerate(((up, up_out), (down, down_out))):
        for h in range(2):
            for j in range(NEAR):
                block = lanes[(2 * h + side) * 32 + j] & (QBLOCKS - 1)
                rows = pl.ds(pl.multiple_of(block * BLOCK, BLOCK), BLOCK)
                for part in range(2):
                    packed[h, part, pl.ds(j * BLOCK, BLOCK), :] = kv[h, part, rows, :]
        send(packed, target)
    for r in range(ROWS // TILE):
        rows = pl.ds(r * TILE, TILE)
        for h in range(2):
            q[h, rows, :] = normed(acc[rows, h * HD : (h + 1) * HD], query_gain[...] * SCALE)
        send(q.at[:, rows], q_out.at[:, rows])
    for copy in copies:
        copy.wait()


def one_hot(rows, lane):
    return (lax.broadcasted_iota(jnp.int32, (rows, HD), 1) == lane).astype(f32).astype(bf16)


def block_bias(mask, slot):
    frame = lax.axis_index("frame")
    lane = lax.broadcasted_iota(jnp.int32, (QBLOCKS, HD), 1)
    table = mask[slot].astype(f32)
    table = jnp.where((lane < QBLOCKS) & (frame == 0), 0.0, table)
    table = jnp.where((lane >= 2 * QBLOCKS) & (frame == FRAMES - 1), 0.0, table)
    return (table - 1.0) * -BLOCKED


def attend_tile(q, bias, keys, vals, h, t, total):
    per = TILE // BLOCK
    rows = [jnp.broadcast_to(bias[t * per + i : t * per + i + 1], (BLOCK, HD)) for i in range(per)]
    query = jnp.concatenate([q[h, pl.ds(t * TILE, TILE), :], jnp.concatenate(rows, axis=0).astype(bf16)], axis=1)
    width = 512
    for c in range(keys.shape[1] // width):
        part = pl.ds(c * width, width)
        scores = lax.dot_general(query, keys[h, part, :], (((1,), (1,)), ((), ())), preferred_element_type=f32)
        weight = jnp.exp2(scores).astype(bf16)
        product = jnp.dot(weight, vals[h, part, :], preferred_element_type=f32)
        total = product if total is None else total + product
    return total


def attend_own(labels, mask, q, kv, after, totals, keys, vals):
    _, *slots = slots_of(labels)
    for b in range(QBLOCKS):
        own = one_hot(BLOCK, QBLOCKS + b)
        for h in range(2):
            keys[h, pl.ds(b * BLOCK, BLOCK), HD:] = own
    for h in range(2):
        keys[h, :, 0:HD] = kv[h, 0]
        vals[h, :, 0:HD] = kv[h, 1]
        vals[h, :, HD:] = jnp.ones((ROWS, HD), bf16)
    for h in range(2):
        bias = block_bias(mask, slots[h])
        for t in range(ROWS // TILE):
            totals[h, pl.ds(t * TILE, TILE), :] = attend_tile(q, bias, keys, vals, h, t, None)


def attend_near(labels, lanes, mask, q, totals, below, above, out, keys, vals):
    _, *slots = slots_of(labels)
    near = NEAR * BLOCK
    per_target = ROWS // GROUPS
    for h in range(2):
        vals[h, :, HD:] = jnp.ones((2 * near, HD), bf16)
        for side, got in enumerate((below, above)):
            rows = pl.ds(side * near, near)
            keys[h, rows, 0:HD] = got[h, 0]
            vals[h, rows, 0:HD] = got[h, 1]
            for j in range(NEAR):
                lane = lanes[(2 * h + side) * 32 + j]
                keys[h, pl.ds(side * near + j * BLOCK, BLOCK), HD:] = one_hot(BLOCK, lane)
    for h in range(2):
        bias = block_bias(mask, slots[h])
        for t in range(ROWS // TILE):
            total = attend_tile(q, bias, keys, vals, h, t, totals[h, pl.ds(t * TILE, TILE), :])
            mixed = (total[:, 0:HD] / total[:, HD:]).astype(bf16)
            targets = pl.ds(t * TILE // per_target, TILE // per_target)
            column = pl.ds(pl.multiple_of(slots[h] * HD, HD), HD)
            out[targets, :, column] = mixed.reshape(-1, per_target, HD)


def time_attend(labels, time_mask, got, out, done, made, sems):
    done[...] = jnp.zeros_like(done)
    time, _, _ = slots_of(labels)
    lane = lax.broadcasted_iota(jnp.int32, (16, HD), 1)
    row = lax.broadcasted_iota(jnp.int32, (16, HD), 0)
    same = (lane & 1) == (row >> 3)
    tables = []
    for a in range(4):
        allowed = jnp.zeros((16, HD), jnp.int32)
        for b in range(4):
            allowed = jnp.where((lane >> 1) == b, time_mask[time, a, b], allowed)
        table = jnp.where(same & (allowed == 1), 0.0, BLOCKED).astype(bf16)
        tables.append(jnp.broadcast_to(table[None], (8, 16, HD)))
    bias = jnp.concatenate(tables, axis=0).reshape(512, HD)
    key_frame = lax.broadcasted_iota(jnp.int32, (512, HD), 0)
    key_lane = lax.broadcasted_iota(jnp.int32, (512, HD), 1)
    mark = (((key_frame >> 7) * 2 + ((key_frame >> 3) & 1)) == key_lane).astype(f32).astype(bf16)
    ones = jnp.ones((512, HD), bf16)
    copies = []
    for u in range(2):
        def rows(part):
            return got[:, pl.ds(part * FRAMES + u * 16, 16), :].reshape(512, HD)

        query = jnp.concatenate([rows(0), bias], axis=1)
        keys = jnp.concatenate([rows(1), mark], axis=1)
        vals = jnp.concatenate([rows(2), ones], axis=1)
        scores = lax.dot_general(query, keys, (((1,), (1,)), ((), ())), preferred_element_type=f32)
        weight = jnp.exp2(scores).astype(bf16)
        total = jnp.dot(weight, vals, preferred_element_type=f32)
        mixed = (total[:, 0:HD] / total[:, HD:]).astype(bf16)
        made[u] = mixed.reshape(FRAMES, 16, HD)
        copies.append(pltpu.make_async_copy(made.at[u], out.at[:, pl.ds(u * 16, 16), :], sems.at[u]))
        copies[-1].start()
    for copy in copies:
        copy.wait()


def merge(labels, space, timed, out, sem):
    time, _, _ = slots_of(labels)
    column = pl.ds(pl.multiple_of(time * HD, HD), HD)
    copy = pltpu.make_async_copy(timed, out.at[:, :, column], sem)
    copy.start()
    copy.wait()


def assemble(parts, out, sems):
    width = parts.shape[2]
    copies = [
        pltpu.make_async_copy(parts.at[g], out.at[:, pl.ds(g * width, width)], sems.at[g]) for g in range(GROUPS)
    ]
    for copy in copies:
        copy.start()
    for copy in copies:
        copy.wait()


def params(mib):
    return pltpu.CompilerParams(vmem_limit_bytes=mib * 2**20)


def cost(flops, moved, exps=0):
    return pl.CostEstimate(flops=int(flops), bytes_accessed=int(moved), transcendentals=int(exps))


SMEM = pl.BlockSpec(memory_space=pltpu.SMEM)
VMEM = pl.BlockSpec(memory_space=pltpu.VMEM)
ANY = pl.BlockSpec(memory_space=pl.ANY)


def on_device(tokens, qkv_weight, query_gain, key_gain, labels, space_mask, time_mask):
    gains = (query_gain.reshape(1, HD), key_gain.reshape(1, HD))
    sent = pl.pallas_call(
        time_project,
        out_shape=jax.ShapeDtypeStruct((FRAMES, 3 * FRAMES, HD), bf16),
        in_specs=[SMEM, ANY, ANY, VMEM, VMEM],
        out_specs=ANY,
        scratch_shapes=[
            pltpu.VMEM((FRAMES, 3 * FRAMES, HD), bf16),
            pltpu.VMEM((ROWS, D), bf16),
            pltpu.VMEM((D, 3 * HD), bf16),
            pltpu.VMEM((ROWS, 3 * HD), f32),
            pltpu.SemaphoreType.DMA((PARTS, 4)),
            pltpu.SemaphoreType.DMA((4,)),
        ],
        compiler_params=params(60),
        cost_estimate=cost(2 * ROWS * D * 3 * HD, 9e6),
        name="time_project",
    )(labels, tokens, qkv_weight, *gains)
    got = lax.all_to_all(sent, "frame", split_axis=0, concat_axis=0, tiled=True)

    live = jnp.pad(jnp.max(space_mask, axis=1), ((0, 0), (0, HD - 3 * QBLOCKS)))
    pair = jax.ShapeDtypeStruct((2, 2, NEAR * BLOCK, HD), bf16)
    q, kv, up, down, lanes = pl.pallas_call(
        space_project,
        out_shape=(
            jax.ShapeDtypeStruct((2, ROWS, HD), bf16),
            jax.ShapeDtypeStruct((2, 2, ROWS, HD), bf16),
            pair,
            pair,
            jax.ShapeDtypeStruct((HD,), jnp.int32),
        ),
        in_specs=[SMEM, SMEM, ANY, ANY, VMEM, VMEM],
        out_specs=(ANY, ANY, ANY, ANY, SMEM),
        scratch_shapes=[
            pltpu.VMEM((2, ROWS, HD), bf16),
            pltpu.VMEM((2, 2, ROWS, HD), bf16),
            pltpu.VMEM((2, 2, NEAR * BLOCK, HD), bf16),
            pltpu.VMEM((2, 2, NEAR * BLOCK, HD), bf16),
            pltpu.VMEM((ROWS, D), bf16),
            pltpu.VMEM((D, 6 * HD), bf16),
            pltpu.VMEM((ROWS, 6 * HD), f32),
            pltpu.SemaphoreType.DMA((PARTS, 7)),
            pltpu.SemaphoreType.DMA((10,)),
        ],
        compiler_params=params(58),
        cost_estimate=cost(2 * ROWS * D * 6 * HD, 12e6),
        name="space_project",
    )(labels, live, tokens, qkv_weight, *gains)
    below = lax.ppermute(up, "frame", [(i, i + 1) for i in range(FRAMES - 1)])
    above = lax.ppermute(down, "frame", [(i + 1, i) for i in range(FRAMES - 1)])

    time_out, done = pl.pallas_call(
        time_attend,
        out_shape=(jax.ShapeDtypeStruct((FRAMES, FRAMES, HD), bf16), jax.ShapeDtypeStruct((8, HD), f32)),
        in_specs=[SMEM, SMEM, VMEM],
        out_specs=(ANY, VMEM),
        scratch_shapes=[pltpu.VMEM((2, FRAMES, 16, HD), bf16), pltpu.SemaphoreType.DMA((2,))],
        compiler_params=params(16),
        cost_estimate=cost(8 * 512 * 512 * 2 * HD, 1e6, 2 * 512 * 512),
        name="time_attend",
    )(labels, time_mask, got)

    mask = jnp.pad(space_mask, ((0, 0), (0, 0), (0, HD - 3 * QBLOCKS)))
    per_target = ROWS // GROUPS
    sides = (2, ROWS, 2 * HD)
    scratch = [pltpu.VMEM(sides, bf16), pltpu.VMEM(sides, bf16)]
    half = cost(2 * 4 * ROWS * ROWS * 2 * HD, 4e6, 2 * ROWS * ROWS)
    totals = pl.pallas_call(
        attend_own,
        out_shape=jax.ShapeDtypeStruct(sides, f32),
        in_specs=[SMEM, VMEM, VMEM, VMEM, ANY],
        out_specs=VMEM,
        scratch_shapes=scratch,
        compiler_params=params(16),
        cost_estimate=half,
        name="attend_own",
    )(labels, mask, q, kv, done)
    space_out = pl.pallas_call(
        attend_near,
        out_shape=jax.ShapeDtypeStruct((GROUPS, per_target, 3 * HD), bf16),
        in_specs=[SMEM, SMEM] + [VMEM] * 5,
        out_specs=VMEM,
        scratch_shapes=scratch,
        compiler_params=params(16),
        cost_estimate=half,
        name="attend_near",
    )(labels, lanes, mask, q, totals, below, above)
    timed = lax.all_to_all(time_out, "frame", split_axis=0, concat_axis=0, tiled=True)
    merged = pl.pallas_call(
        merge,
        out_shape=jax.ShapeDtypeStruct((GROUPS, per_target, 3 * HD), bf16),
        in_specs=[SMEM, ANY, ANY],
        out_specs=ANY,
        scratch_shapes=[pltpu.SemaphoreType.DMA],
        input_output_aliases={1: 0},
        compiler_params=params(16),
        cost_estimate=cost(1, 5e5),
        name="merge",
    )(labels, space_out, timed.reshape(GROUPS, per_target, HD))
    parts = lax.all_to_all(merged, "head", split_axis=0, concat_axis=0, tiled=True)
    return pl.pallas_call(
        assemble,
        out_shape=jax.ShapeDtypeStruct((per_target, 3 * GROUPS * HD), bf16),
        in_specs=[ANY],
        out_specs=ANY,
        scratch_shapes=[pltpu.SemaphoreType.DMA((GROUPS,))],
        compiler_params=params(16),
        cost_estimate=cost(1, 2e6),
        name="assemble",
    )(parts)


def solution(mesh):
    placed = (
        P("frame", None),
        P(None, None, "head"),
        P(),
        P(),
        P("head"),
        P("head", None, None),
        P("head", None, None),
    )
    return jax.shard_map(
        on_device, mesh=mesh, in_specs=placed, out_specs=P(("frame", "head"), None), check_vma=False
    )
```

```python
import math

import jax
import jax.numpy as jnp
from jax import lax
from jax.experimental import pallas as pl
from jax.experimental.pallas import tpu as pltpu
from jax.sharding import PartitionSpec as P

STRIP = 8
BLOCK = 64
D = 3072
HD = 128
ROWS = 1024
FRAMES = 32
GROUPS = 8
QBLOCKS = 16
NEAR = 8
CHUNKS = (512, 768, 768, 768, 256)
STARTS = tuple(sum(CHUNKS[:c]) for c in range(len(CHUNKS)))
PARTS = len(CHUNKS)
TILE = 256
EPSILON = 1e-06
SCALE = math.log2(math.e) / math.sqrt(HD)
BLOCKED = -16384.0
DEAD = 64

bf16 = jnp.bfloat16
f32 = jnp.float32


def slots_of(labels):
    time = labels[1] + 2 * labels[2]
    return time, jnp.where(time == 0, 1, 0), jnp.where(time == 2, 1, 2)


def normed(x, gain):
    inverse = lax.rsqrt(jnp.mean(x * x, axis=-1, keepdims=True) + EPSILON)
    return (x * inverse * gain).astype(bf16)


def project(tokens, weight, columns, tok, wts, acc, sems, meanwhile=None):
    def copies(c):
        part = pl.ds(STARTS[c], CHUNKS[c])
        made = [pltpu.make_async_copy(tokens.at[:, part], tok.at[:, part], sems.at[c, 0])]
        for i, (k, slot) in enumerate(columns):
            column = pl.ds(pl.multiple_of(slot * HD, HD), HD)
            made.append(
                pltpu.make_async_copy(weight.at[k, part, column], wts.at[part, pl.ds(i * HD, HD)], sems.at[c, 1 + i])
            )
        return made

    for c in range(2):
        for copy in copies(c):
            copy.start()
    if meanwhile is not None:
        meanwhile()
    for c in range(PARTS):
        for copy in copies(c):
            copy.wait()
        if c + 2 < PARTS:
            for copy in copies(c + 2):
                copy.start()
        part = pl.ds(STARTS[c], CHUNKS[c])
        product = jnp.dot(tok[:, part], wts[part, :], preferred_element_type=f32)
        if c == 0:
            acc[...] = product
        else:
            acc[...] += product


def time_project(labels, tokens, weight, query_gain, key_gain, out, made, tok, wts, acc, sems, out_sems):
    time, _, _ = slots_of(labels)
    project(tokens, weight, [(0, time), (1, time), (2, time)], tok, wts, acc, sems)
    copies = []
    for b in range(FRAMES):
        rows = pl.ds(b * FRAMES, FRAMES)
        owner = FRAMES - 1 - b
        made[owner, 0:FRAMES, :] = normed(acc[rows, 0:HD], query_gain[...] * SCALE)
        made[owner, FRAMES : 2 * FRAMES, :] = normed(acc[rows, HD : 2 * HD], key_gain[...])
        made[owner, 2 * FRAMES :, :] = acc[rows, 2 * HD :].astype(bf16)
        if b % 8 == 7:
            group = pl.ds(owner, 8)
            copies.append(pltpu.make_async_copy(made.at[group], out.at[group], out_sems.at[b // 8]))
            copies[-1].start()
    for copy in copies:
        copy.wait()


def list_near(labels, live, lanes):
    _, *slots = slots_of(labels)
    for h in range(2):
        for side in range(2):
            base = (2 * h + side) * 32
            for j in range(32):
                lanes[base + j] = DEAD
            count = 0
            for b in range(QBLOCKS):
                column = 2 * QBLOCKS * side + b
                alive = live[slots[h], column] > 0
                lanes[base + count] = jnp.where(alive, column, DEAD)
                count = count + alive.astype(jnp.int32)


def space_project(labels, live, tokens, weight, query_gain, key_gain, *rest):
    q_out, kv_out, up_out, down_out, lanes, q, kv, up, down, tok, wts, acc, sems, out_sems = rest
    _, first, second = slots_of(labels)
    columns = [(k, slot) for k in range(3) for slot in (first, second)]
    project(tokens, weight, columns, tok, wts, acc, sems, lambda: list_near(labels, live, lanes))
    copies = []

    def send(source, target):
        copies.append(pltpu.make_async_copy(source, target, out_sems.at[len(copies)]))
        copies[-1].start()

    for r in range(ROWS // TILE):
        rows = pl.ds(r * TILE, TILE)
        for h in range(2):
            kv[h, 0, rows, :] = normed(acc[rows, (2 + h) * HD : (3 + h) * HD], key_gain[...])
            kv[h, 1, rows, :] = acc[rows, (4 + h) * HD : (5 + h) * HD].astype(bf16)
        send(kv.at[:, :, rows], kv_out.at[:, :, rows])
    for side, (packed, target) in enumerate(((up, up_out), (down, down_out))):
        for h in range(2):
            for j in range(NEAR):
                block = lanes[(2 * h + side) * 32 + j] & (QBLOCKS - 1)
                rows = pl.ds(pl.multiple_of(block * BLOCK, BLOCK), BLOCK)
                for part in range(2):
                    packed[h, part, pl.ds(j * BLOCK, BLOCK), :] = kv[h, part, rows, :]
        send(packed, target)
    for r in range(ROWS // TILE):
        rows = pl.ds(r * TILE, TILE)
        for h in range(2):
            q[h, rows, :] = normed(acc[rows, h * HD : (h + 1) * HD], query_gain[...] * SCALE)
        send(q.at[:, rows], q_out.at[:, rows])
    for copy in copies:
        copy.wait()


def one_hot(rows, lane):
    return (lax.broadcasted_iota(jnp.int32, (rows, HD), 1) == lane).astype(f32).astype(bf16)


def block_bias(mask, slot):
    frame = lax.axis_index("frame")
    lane = lax.broadcasted_iota(jnp.int32, (QBLOCKS, HD), 1)
    table = mask[slot].astype(f32)
    table = jnp.where((lane < QBLOCKS) & (frame == 0), 0.0, table)
    table = jnp.where((lane >= 2 * QBLOCKS) & (frame == FRAMES - 1), 0.0, table)
    return (table - 1.0) * -BLOCKED


def attend_tile(q, bias, keys, vals, h, t, total):
    per = TILE // BLOCK
    rows = [jnp.broadcast_to(bias[t * per + i : t * per + i + 1], (BLOCK, HD)) for i in range(per)]
    query = jnp.concatenate([q[h, pl.ds(t * TILE, TILE), :], jnp.concatenate(rows, axis=0).astype(bf16)], axis=1)
    width = 512
    for c in range(keys.shape[1] // width):
        part = pl.ds(c * width, width)
        scores = lax.dot_general(query, keys[h, part, :], (((1,), (1,)), ((), ())), preferred_element_type=f32)
        weight = jnp.exp2(scores).astype(bf16)
        product = jnp.dot(weight, vals[h, part, :], preferred_element_type=f32)
        total = product if total is None else total + product
    return total


def attend_own(labels, mask, q, kv, after, totals, keys, vals):
    _, *slots = slots_of(labels)
    for b in range(QBLOCKS):
        own = one_hot(BLOCK, QBLOCKS + b)
        for h in range(2):
            keys[h, pl.ds(b * BLOCK, BLOCK), HD:] = own
    for h in range(2):
        keys[h, :, 0:HD] = kv[h, 0]
        vals[h, :, 0:HD] = kv[h, 1]
        vals[h, :, HD:] = jnp.ones((ROWS, HD), bf16)
    for h in range(2):
        bias = block_bias(mask, slots[h])
        for t in range(ROWS // TILE):
            totals[h, pl.ds(t * TILE, TILE), :] = attend_tile(q, bias, keys, vals, h, t, None)


def attend_near(labels, lanes, mask, q, totals, below, above, out, keys, vals):
    _, *slots = slots_of(labels)
    near = NEAR * BLOCK
    per_target = ROWS // GROUPS
    for h in range(2):
        vals[h, :, HD:] = jnp.ones((2 * near, HD), bf16)
        for side, got in enumerate((below, above)):
            rows = pl.ds(side * near, near)
            keys[h, rows, 0:HD] = got[h, 0]
            vals[h, rows, 0:HD] = got[h, 1]
            for j in range(NEAR):
                lane = lanes[(2 * h + side) * 32 + j]
                keys[h, pl.ds(side * near + j * BLOCK, BLOCK), HD:] = one_hot(BLOCK, lane)
    for h in range(2):
        bias = block_bias(mask, slots[h])
        for t in range(ROWS // TILE):
            total = attend_tile(q, bias, keys, vals, h, t, totals[h, pl.ds(t * TILE, TILE), :])
            mixed = (total[:, 0:HD] / total[:, HD:]).astype(bf16)
            targets = pl.ds(t * TILE // per_target, TILE // per_target)
            column = pl.ds(pl.multiple_of(slots[h] * HD, HD), HD)
            out[targets, :, column] = mixed.reshape(-1, per_target, HD)


def time_attend(labels, time_mask, got, out, done, made, sems):
    done[...] = jnp.zeros_like(done)
    time, _, _ = slots_of(labels)
    lane = lax.broadcasted_iota(jnp.int32, (16, HD), 1)
    row = lax.broadcasted_iota(jnp.int32, (16, HD), 0)
    same = (lane & 1) == (row >> 3)
    tables = []
    for a in range(4):
        allowed = jnp.zeros((16, HD), jnp.int32)
        for b in range(4):
            allowed = jnp.where((lane >> 1) == b, time_mask[time, a, b], allowed)
        table = jnp.where(same & (allowed == 1), 0.0, BLOCKED).astype(bf16)
        tables.append(jnp.broadcast_to(table[None], (8, 16, HD)))
    bias = jnp.concatenate(tables, axis=0).reshape(512, HD)
    key_frame = lax.broadcasted_iota(jnp.int32, (512, HD), 0)
    key_lane = lax.broadcasted_iota(jnp.int32, (512, HD), 1)
    mark = (((key_frame >> 7) * 2 + ((key_frame >> 3) & 1)) == key_lane).astype(f32).astype(bf16)
    ones = jnp.ones((512, HD), bf16)
    copies = []
    for u in range(2):
        def rows(part):
            return got[:, pl.ds(part * FRAMES + u * 16, 16), :].reshape(512, HD)

        query = jnp.concatenate([rows(0), bias], axis=1)
        keys = jnp.concatenate([rows(1), mark], axis=1)
        vals = jnp.concatenate([rows(2), ones], axis=1)
        scores = lax.dot_general(query, keys, (((1,), (1,)), ((), ())), preferred_element_type=f32)
        weight = jnp.exp2(scores).astype(bf16)
        total = jnp.dot(weight, vals, preferred_element_type=f32)
        mixed = (total[:, 0:HD] / total[:, HD:]).astype(bf16)
        for f in range(FRAMES):
            made[u, FRAMES - 1 - f] = mixed[f * 16 : (f + 1) * 16]
        copies.append(pltpu.make_async_copy(made.at[u], out.at[:, pl.ds(u * 16, 16), :], sems.at[u]))
        copies[-1].start()
    for copy in copies:
        copy.wait()


def merge(labels, space, timed, out, sem):
    time, _, _ = slots_of(labels)
    column = pl.ds(pl.multiple_of(time * HD, HD), HD)
    copy = pltpu.make_async_copy(timed, out.at[:, :, column], sem)
    copy.start()
    copy.wait()


def assemble(parts, out, sems):
    width = parts.shape[2]
    copies = [
        pltpu.make_async_copy(parts.at[g], out.at[:, pl.ds(g * width, width)], sems.at[g]) for g in range(GROUPS)
    ]
    for copy in copies:
        copy.start()
    for copy in copies:
        copy.wait()


def params(mib):
    return pltpu.CompilerParams(vmem_limit_bytes=mib * 2**20)


def cost(flops, moved, exps=0):
    return pl.CostEstimate(flops=int(flops), bytes_accessed=int(moved), transcendentals=int(exps))


SMEM = pl.BlockSpec(memory_space=pltpu.SMEM)
VMEM = pl.BlockSpec(memory_space=pltpu.VMEM)
ANY = pl.BlockSpec(memory_space=pl.ANY)


def on_device(tokens, qkv_weight, query_gain, key_gain, labels, space_mask, time_mask):
    gains = (query_gain.reshape(1, HD), key_gain.reshape(1, HD))
    sent = pl.pallas_call(
        time_project,
        out_shape=jax.ShapeDtypeStruct((FRAMES, 3 * FRAMES, HD), bf16),
        in_specs=[SMEM, ANY, ANY, VMEM, VMEM],
        out_specs=ANY,
        scratch_shapes=[
            pltpu.VMEM((FRAMES, 3 * FRAMES, HD), bf16),
            pltpu.VMEM((ROWS, D), bf16),
            pltpu.VMEM((D, 3 * HD), bf16),
            pltpu.VMEM((ROWS, 3 * HD), f32),
            pltpu.SemaphoreType.DMA((PARTS, 4)),
            pltpu.SemaphoreType.DMA((4,)),
        ],
        compiler_params=params(60),
        cost_estimate=cost(2 * ROWS * D * 3 * HD, 9e6),
        name="time_project",
    )(labels, tokens, qkv_weight, *gains)
    got = lax.all_to_all(sent, "frame", split_axis=0, concat_axis=0, tiled=True)

    live = jnp.pad(jnp.max(space_mask, axis=1), ((0, 0), (0, HD - 3 * QBLOCKS)))
    pair = jax.ShapeDtypeStruct((2, 2, NEAR * BLOCK, HD), bf16)
    q, kv, up, down, lanes = pl.pallas_call(
        space_project,
        out_shape=(
            jax.ShapeDtypeStruct((2, ROWS, HD), bf16),
            jax.ShapeDtypeStruct((2, 2, ROWS, HD), bf16),
            pair,
            pair,
            jax.ShapeDtypeStruct((HD,), jnp.int32),
        ),
        in_specs=[SMEM, SMEM, ANY, ANY, VMEM, VMEM],
        out_specs=(ANY, ANY, ANY, ANY, SMEM),
        scratch_shapes=[
            pltpu.VMEM((2, ROWS, HD), bf16),
            pltpu.VMEM((2, 2, ROWS, HD), bf16),
            pltpu.VMEM((2, 2, NEAR * BLOCK, HD), bf16),
            pltpu.VMEM((2, 2, NEAR * BLOCK, HD), bf16),
            pltpu.VMEM((ROWS, D), bf16),
            pltpu.VMEM((D, 6 * HD), bf16),
            pltpu.VMEM((ROWS, 6 * HD), f32),
            pltpu.SemaphoreType.DMA((PARTS, 7)),
            pltpu.SemaphoreType.DMA((10,)),
        ],
        compiler_params=params(58),
        cost_estimate=cost(2 * ROWS * D * 6 * HD, 12e6),
        name="space_project",
    )(labels, live, tokens, qkv_weight, *gains)
    below = lax.ppermute(up, "frame", [(i, i + 1) for i in range(FRAMES - 1)])
    above = lax.ppermute(down, "frame", [(i + 1, i) for i in range(FRAMES - 1)])

    time_out, done = pl.pallas_call(
        time_attend,
        out_shape=(jax.ShapeDtypeStruct((FRAMES, FRAMES, HD), bf16), jax.ShapeDtypeStruct((8, HD), f32)),
        in_specs=[SMEM, SMEM, VMEM],
        out_specs=(ANY, VMEM),
        scratch_shapes=[pltpu.VMEM((2, FRAMES, 16, HD), bf16), pltpu.SemaphoreType.DMA((2,))],
        compiler_params=params(16),
        cost_estimate=cost(8 * 512 * 512 * 2 * HD, 1e6, 2 * 512 * 512),
        name="time_attend",
    )(labels, time_mask, got)

    mask = jnp.pad(space_mask, ((0, 0), (0, 0), (0, HD - 3 * QBLOCKS)))
    per_target = ROWS // GROUPS
    sides = (2, ROWS, 2 * HD)
    scratch = [pltpu.VMEM(sides, bf16), pltpu.VMEM(sides, bf16)]
    half = cost(2 * 4 * ROWS * ROWS * 2 * HD, 4e6, 2 * ROWS * ROWS)
    totals = pl.pallas_call(
        attend_own,
        out_shape=jax.ShapeDtypeStruct(sides, f32),
        in_specs=[SMEM, VMEM, VMEM, VMEM, ANY],
        out_specs=VMEM,
        scratch_shapes=scratch,
        compiler_params=params(16),
        cost_estimate=half,
        name="attend_own",
    )(labels, mask, q, kv, done)
    space_out = pl.pallas_call(
        attend_near,
        out_shape=jax.ShapeDtypeStruct((GROUPS, per_target, 3 * HD), bf16),
        in_specs=[SMEM, SMEM] + [VMEM] * 5,
        out_specs=VMEM,
        scratch_shapes=scratch,
        compiler_params=params(16),
        cost_estimate=half,
        name="attend_near",
    )(labels, lanes, mask, q, totals, below, above)
    backwards = [list(range(FRAMES - 1, -1, -1))]
    timed = lax.all_to_all(
        time_out, "frame", split_axis=0, concat_axis=0, tiled=True, axis_index_groups=backwards
    )
    merged = pl.pallas_call(
        merge,
        out_shape=jax.ShapeDtypeStruct((GROUPS, per_target, 3 * HD), bf16),
        in_specs=[SMEM, ANY, ANY],
        out_specs=ANY,
        scratch_shapes=[pltpu.SemaphoreType.DMA],
        input_output_aliases={1: 0},
        compiler_params=params(16),
        cost_estimate=cost(1, 5e5),
        name="merge",
    )(labels, space_out, timed.reshape(GROUPS, per_target, HD))
    parts = lax.all_to_all(merged, "head", split_axis=0, concat_axis=0, tiled=True)
    return pl.pallas_call(
        assemble,
        out_shape=jax.ShapeDtypeStruct((per_target, 3 * GROUPS * HD), bf16),
        in_specs=[ANY],
        out_specs=ANY,
        scratch_shapes=[pltpu.SemaphoreType.DMA((GROUPS,))],
        compiler_params=params(16),
        cost_estimate=cost(1, 2e6),
        name="assemble",
    )(parts)


def solution(mesh):
    placed = (
        P("frame", None),
        P(None, None, "head"),
        P(),
        P(),
        P("head"),
        P("head", None, None),
        P("head", None, None),
    )
    return jax.shard_map(
        on_device, mesh=mesh, in_specs=placed, out_specs=P(("frame", "head"), None), check_vma=False
    )
```

```python
import math

import jax
import jax.numpy as jnp
from jax import lax
from jax.experimental import pallas as pl
from jax.experimental.pallas import tpu as pltpu
from jax.sharding import PartitionSpec as P

STRIP = 8
BLOCK = 64
D = 3072
HD = 128
ROWS = 1024
FRAMES = 32
GROUPS = 8
QBLOCKS = 16
NEAR = 8
CHUNKS = (512, 768, 768, 768, 256)
STARTS = tuple(sum(CHUNKS[:c]) for c in range(len(CHUNKS)))
PARTS = len(CHUNKS)
TILE = 256
EPSILON = 1e-06
SCALE = math.log2(math.e) / math.sqrt(HD)
BLOCKED = -16384.0
DEAD = 64

bf16 = jnp.bfloat16
f32 = jnp.float32


def slots_of(labels):
    time = labels[1] + 2 * labels[2]
    return time, jnp.where(time == 0, 1, 0), jnp.where(time == 2, 1, 2)


def normed(x, gain):
    inverse = lax.rsqrt(jnp.mean(x * x, axis=-1, keepdims=True) + EPSILON)
    return (x * inverse * gain).astype(bf16)


def project(tokens, weight, columns, tok, wts, acc, sems, meanwhile=None):
    def copies(c):
        part = pl.ds(STARTS[c], CHUNKS[c])
        made = [pltpu.make_async_copy(tokens.at[:, part], tok.at[:, part], sems.at[c, 0])]
        for i, (k, slot) in enumerate(columns):
            column = pl.ds(pl.multiple_of(slot * HD, HD), HD)
            made.append(
                pltpu.make_async_copy(weight.at[k, part, column], wts.at[part, pl.ds(i * HD, HD)], sems.at[c, 1 + i])
            )
        return made

    for c in range(2):
        for copy in copies(c):
            copy.start()
    if meanwhile is not None:
        meanwhile()
    for c in range(PARTS):
        for copy in copies(c):
            copy.wait()
        if c + 2 < PARTS:
            for copy in copies(c + 2):
                copy.start()
        part = pl.ds(STARTS[c], CHUNKS[c])
        product = jnp.dot(tok[:, part], wts[part, :], preferred_element_type=f32)
        if c == 0:
            acc[...] = product
        else:
            acc[...] += product


def time_project(labels, tokens, weight, query_gain, key_gain, out, made, tok, wts, acc, sems, out_sems):
    time, _, _ = slots_of(labels)
    project(tokens, weight, [(0, time), (1, time), (2, time)], tok, wts, acc, sems)
    copies = []
    for b in range(FRAMES):
        rows = pl.ds(b * FRAMES, FRAMES)
        made[b, 0:FRAMES, :] = normed(acc[rows, 0:HD], query_gain[...])
        made[b, FRAMES : 2 * FRAMES, :] = normed(acc[rows, HD : 2 * HD], key_gain[...])
        made[b, 2 * FRAMES :, :] = acc[rows, 2 * HD :].astype(bf16)
        if b % 8 == 7:
            group = pl.ds(b - 7, 8)
            copies.append(pltpu.make_async_copy(made.at[group], out.at[group], out_sems.at[b // 8]))
            copies[-1].start()
    for copy in copies:
        copy.wait()


def list_near(labels, live, lanes):
    _, *slots = slots_of(labels)
    for h in range(2):
        for side in range(2):
            base = (2 * h + side) * 32
            for j in range(32):
                lanes[base + j] = DEAD
            count = 0
            for b in range(QBLOCKS):
                column = 2 * QBLOCKS * side + b
                alive = live[slots[h], column] > 0
                lanes[base + count] = jnp.where(alive, column, DEAD)
                count = count + alive.astype(jnp.int32)


def space_project(labels, live, tokens, weight, query_gain, key_gain, *rest):
    q_out, kv_out, up_out, down_out, lanes, q, kv, up, down, tok, wts, acc, sems, out_sems = rest
    _, first, second = slots_of(labels)
    columns = [(k, slot) for k in range(3) for slot in (first, second)]
    project(tokens, weight, columns, tok, wts, acc, sems, lambda: list_near(labels, live, lanes))
    copies = []

    def send(source, target):
        copies.append(pltpu.make_async_copy(source, target, out_sems.at[len(copies)]))
        copies[-1].start()

    for r in range(ROWS // TILE):
        rows = pl.ds(r * TILE, TILE)
        for h in range(2):
            kv[h, 0, rows, :] = normed(acc[rows, (2 + h) * HD : (3 + h) * HD], key_gain[...])
            kv[h, 1, rows, :] = acc[rows, (4 + h) * HD : (5 + h) * HD].astype(bf16)
        send(kv.at[:, :, rows], kv_out.at[:, :, rows])
    for side, (packed, target) in enumerate(((up, up_out), (down, down_out))):
        for h in range(2):
            for j in range(NEAR):
                block = lanes[(2 * h + side) * 32 + j] & (QBLOCKS - 1)
                rows = pl.ds(pl.multiple_of(block * BLOCK, BLOCK), BLOCK)
                for part in range(2):
                    packed[h, part, pl.ds(j * BLOCK, BLOCK), :] = kv[h, part, rows, :]
        send(packed, target)
    for r in range(ROWS // TILE):
        rows = pl.ds(r * TILE, TILE)
        for h in range(2):
            q[h, rows, :] = normed(acc[rows, h * HD : (h + 1) * HD], query_gain[...])
        send(q.at[:, rows], q_out.at[:, rows])
    for copy in copies:
        copy.wait()


def one_hot(rows, lane):
    return (lax.broadcasted_iota(jnp.int32, (rows, HD), 1) == lane).astype(f32).astype(bf16)


def block_bias(mask, slot):
    frame = lax.axis_index("frame")
    lane = lax.broadcasted_iota(jnp.int32, (QBLOCKS, HD), 1)
    table = mask[slot].astype(f32)
    table = jnp.where((lane < QBLOCKS) & (frame == 0), 0.0, table)
    table = jnp.where((lane >= 2 * QBLOCKS) & (frame == FRAMES - 1), 0.0, table)
    return (table - 1.0) * -BLOCKED


def attend_tile(q, bias, keys, vals, h, t, total):
    per = TILE // BLOCK
    rows = [jnp.broadcast_to(bias[t * per + i : t * per + i + 1], (BLOCK, HD)) for i in range(per)]
    query = jnp.concatenate([q[h, pl.ds(t * TILE, TILE), :], jnp.concatenate(rows, axis=0).astype(bf16)], axis=1)
    width = 512
    for c in range(keys.shape[1] // width):
        part = pl.ds(c * width, width)
        scores = lax.dot_general(query, keys[h, part, :], (((1,), (1,)), ((), ())), preferred_element_type=f32)
        weight = jnp.exp2(scores * SCALE).astype(bf16)
        product = jnp.dot(weight, vals[h, part, :], preferred_element_type=f32)
        total = product if total is None else total + product
    return total


def attend_own(labels, mask, q, kv, after, totals, keys, vals):
    _, *slots = slots_of(labels)
    for b in range(QBLOCKS):
        own = one_hot(BLOCK, QBLOCKS + b)
        for h in range(2):
            keys[h, pl.ds(b * BLOCK, BLOCK), HD:] = own
    for h in range(2):
        keys[h, :, 0:HD] = kv[h, 0]
        vals[h, :, 0:HD] = kv[h, 1]
        vals[h, :, HD:] = jnp.ones((ROWS, HD), bf16)
    for h in range(2):
        bias = block_bias(mask, slots[h])
        for t in range(ROWS // TILE):
            totals[h, pl.ds(t * TILE, TILE), :] = attend_tile(q, bias, keys, vals, h, t, None)


def attend_near(labels, lanes, mask, q, totals, below, above, out, keys, vals):
    _, *slots = slots_of(labels)
    near = NEAR * BLOCK
    per_target = ROWS // GROUPS
    for h in range(2):
        vals[h, :, HD:] = jnp.ones((2 * near, HD), bf16)
        for side, got in enumerate((below, above)):
            rows = pl.ds(side * near, near)
            keys[h, rows, 0:HD] = got[h, 0]
            vals[h, rows, 0:HD] = got[h, 1]
            for j in range(NEAR):
                lane = lanes[(2 * h + side) * 32 + j]
                keys[h, pl.ds(side * near + j * BLOCK, BLOCK), HD:] = one_hot(BLOCK, lane)
    for h in range(2):
        bias = block_bias(mask, slots[h])
        for t in range(ROWS // TILE):
            total = attend_tile(q, bias, keys, vals, h, t, totals[h, pl.ds(t * TILE, TILE), :])
            mixed = (total[:, 0:HD] / total[:, HD:]).astype(bf16)
            targets = pl.ds(t * TILE // per_target, TILE // per_target)
            column = pl.ds(pl.multiple_of(slots[h] * HD, HD), HD)
            out[targets, :, column] = mixed.reshape(-1, per_target, HD)


def time_attend(labels, time_mask, got, out, done, made, sems):
    done[...] = jnp.zeros_like(done)
    time, _, _ = slots_of(labels)
    lane = lax.broadcasted_iota(jnp.int32, (16, HD), 1)
    row = lax.broadcasted_iota(jnp.int32, (16, HD), 0)
    same = (lane & 1) == (row >> 3)
    tables = []
    for a in range(4):
        allowed = jnp.zeros((16, HD), jnp.int32)
        for b in range(4):
            allowed = jnp.where((lane >> 1) == b, time_mask[time, a, b], allowed)
        table = jnp.where(same & (allowed == 1), 0.0, BLOCKED).astype(bf16)
        tables.append(jnp.broadcast_to(table[None], (8, 16, HD)))
    bias = jnp.concatenate(tables, axis=0).reshape(512, HD)
    key_frame = lax.broadcasted_iota(jnp.int32, (512, HD), 0)
    key_lane = lax.broadcasted_iota(jnp.int32, (512, HD), 1)
    mark = (((key_frame >> 7) * 2 + ((key_frame >> 3) & 1)) == key_lane).astype(f32).astype(bf16)
    ones = jnp.ones((512, HD), bf16)
    copies = []
    for u in range(2):
        def rows(part):
            return got[:, pl.ds(part * FRAMES + u * 16, 16), :].reshape(512, HD)

        query = jnp.concatenate([rows(0), bias], axis=1)
        keys = jnp.concatenate([rows(1), mark], axis=1)
        vals = jnp.concatenate([rows(2), ones], axis=1)
        scores = lax.dot_general(query, keys, (((1,), (1,)), ((), ())), preferred_element_type=f32)
        weight = jnp.exp2(scores * SCALE).astype(bf16)
        total = jnp.dot(weight, vals, preferred_element_type=f32)
        mixed = (total[:, 0:HD] / total[:, HD:]).astype(bf16)
        made[u] = mixed.reshape(FRAMES, 16, HD)
        copies.append(pltpu.make_async_copy(made.at[u], out.at[:, pl.ds(u * 16, 16), :], sems.at[u]))
        copies[-1].start()
    for copy in copies:
        copy.wait()


def merge(labels, space, timed, out, sem):
    time, _, _ = slots_of(labels)
    column = pl.ds(pl.multiple_of(time * HD, HD), HD)
    copy = pltpu.make_async_copy(timed, out.at[:, :, column], sem)
    copy.start()
    copy.wait()


def assemble(parts, out, sems):
    width = parts.shape[2]
    copies = [
        pltpu.make_async_copy(parts.at[g], out.at[:, pl.ds(g * width, width)], sems.at[g]) for g in range(GROUPS)
    ]
    for copy in copies:
        copy.start()
    for copy in copies:
        copy.wait()


def params(mib):
    return pltpu.CompilerParams(vmem_limit_bytes=mib * 2**20)


def cost(flops, moved, exps=0):
    return pl.CostEstimate(flops=int(flops), bytes_accessed=int(moved), transcendentals=int(exps))


SMEM = pl.BlockSpec(memory_space=pltpu.SMEM)
VMEM = pl.BlockSpec(memory_space=pltpu.VMEM)
ANY = pl.BlockSpec(memory_space=pl.ANY)


def on_device(tokens, qkv_weight, query_gain, key_gain, labels, space_mask, time_mask):
    gains = (query_gain.reshape(1, HD), key_gain.reshape(1, HD))
    sent = pl.pallas_call(
        time_project,
        out_shape=jax.ShapeDtypeStruct((FRAMES, 3 * FRAMES, HD), bf16),
        in_specs=[SMEM, ANY, ANY, VMEM, VMEM],
        out_specs=ANY,
        scratch_shapes=[
            pltpu.VMEM((FRAMES, 3 * FRAMES, HD), bf16),
            pltpu.VMEM((ROWS, D), bf16),
            pltpu.VMEM((D, 3 * HD), bf16),
            pltpu.VMEM((ROWS, 3 * HD), f32),
            pltpu.SemaphoreType.DMA((PARTS, 4)),
            pltpu.SemaphoreType.DMA((4,)),
        ],
        compiler_params=params(60),
        cost_estimate=cost(2 * ROWS * D * 3 * HD, 9e6),
        name="time_project",
    )(labels, tokens, qkv_weight, *gains)
    got = lax.all_to_all(sent, "frame", split_axis=0, concat_axis=0, tiled=True)

    live = jnp.pad(jnp.max(space_mask, axis=1), ((0, 0), (0, HD - 3 * QBLOCKS)))
    pair = jax.ShapeDtypeStruct((2, 2, NEAR * BLOCK, HD), bf16)
    q, kv, up, down, lanes = pl.pallas_call(
        space_project,
        out_shape=(
            jax.ShapeDtypeStruct((2, ROWS, HD), bf16),
            jax.ShapeDtypeStruct((2, 2, ROWS, HD), bf16),
            pair,
            pair,
            jax.ShapeDtypeStruct((HD,), jnp.int32),
        ),
        in_specs=[SMEM, SMEM, ANY, ANY, VMEM, VMEM],
        out_specs=(ANY, ANY, ANY, ANY, SMEM),
        scratch_shapes=[
            pltpu.VMEM((2, ROWS, HD), bf16),
            pltpu.VMEM((2, 2, ROWS, HD), bf16),
            pltpu.VMEM((2, 2, NEAR * BLOCK, HD), bf16),
            pltpu.VMEM((2, 2, NEAR * BLOCK, HD), bf16),
            pltpu.VMEM((ROWS, D), bf16),
            pltpu.VMEM((D, 6 * HD), bf16),
            pltpu.VMEM((ROWS, 6 * HD), f32),
            pltpu.SemaphoreType.DMA((PARTS, 7)),
            pltpu.SemaphoreType.DMA((10,)),
        ],
        compiler_params=params(58),
        cost_estimate=cost(2 * ROWS * D * 6 * HD, 12e6),
        name="space_project",
    )(labels, live, tokens, qkv_weight, *gains)
    below = lax.ppermute(up, "frame", [(i, i + 1) for i in range(FRAMES - 1)])
    above = lax.ppermute(down, "frame", [(i + 1, i) for i in range(FRAMES - 1)])

    time_out, done = pl.pallas_call(
        time_attend,
        out_shape=(jax.ShapeDtypeStruct((FRAMES, FRAMES, HD), bf16), jax.ShapeDtypeStruct((8, HD), f32)),
        in_specs=[SMEM, SMEM, VMEM],
        out_specs=(ANY, VMEM),
        scratch_shapes=[pltpu.VMEM((2, FRAMES, 16, HD), bf16), pltpu.SemaphoreType.DMA((2,))],
        compiler_params=params(16),
        cost_estimate=cost(8 * 512 * 512 * 2 * HD, 1e6, 2 * 512 * 512),
        name="time_attend",
    )(labels, time_mask, got)

    mask = jnp.pad(space_mask, ((0, 0), (0, 0), (0, HD - 3 * QBLOCKS)))
    per_target = ROWS // GROUPS
    sides = (2, ROWS, 2 * HD)
    scratch = [pltpu.VMEM(sides, bf16), pltpu.VMEM(sides, bf16)]
    half = cost(2 * 4 * ROWS * ROWS * 2 * HD, 4e6, 2 * ROWS * ROWS)
    totals = pl.pallas_call(
        attend_own,
        out_shape=jax.ShapeDtypeStruct(sides, f32),
        in_specs=[SMEM, VMEM, VMEM, VMEM, ANY],
        out_specs=VMEM,
        scratch_shapes=scratch,
        compiler_params=params(16),
        cost_estimate=half,
        name="attend_own",
    )(labels, mask, q, kv, done)
    space_out = pl.pallas_call(
        attend_near,
        out_shape=jax.ShapeDtypeStruct((GROUPS, per_target, 3 * HD), bf16),
        in_specs=[SMEM, SMEM] + [VMEM] * 5,
        out_specs=VMEM,
        scratch_shapes=scratch,
        compiler_params=params(16),
        cost_estimate=half,
        name="attend_near",
    )(labels, lanes, mask, q, totals, below, above)
    timed = lax.all_to_all(time_out, "frame", split_axis=0, concat_axis=0, tiled=True)
    merged = pl.pallas_call(
        merge,
        out_shape=jax.ShapeDtypeStruct((GROUPS, per_target, 3 * HD), bf16),
        in_specs=[SMEM, ANY, ANY],
        out_specs=ANY,
        scratch_shapes=[pltpu.SemaphoreType.DMA],
        input_output_aliases={1: 0},
        compiler_params=params(16),
        cost_estimate=cost(1, 5e5),
        name="merge",
    )(labels, space_out, timed.reshape(GROUPS, per_target, HD))
    parts = lax.all_to_all(merged, "head", split_axis=0, concat_axis=0, tiled=True)
    return pl.pallas_call(
        assemble,
        out_shape=jax.ShapeDtypeStruct((per_target, 3 * GROUPS * HD), bf16),
        in_specs=[ANY],
        out_specs=ANY,
        scratch_shapes=[pltpu.SemaphoreType.DMA((GROUPS,))],
        compiler_params=params(16),
        cost_estimate=cost(1, 2e6),
        name="assemble",
    )(parts)


def solution(mesh):
    placed = (
        P("frame", None),
        P(None, None, "head"),
        P(),
        P(),
        P("head"),
        P("head", None, None),
        P("head", None, None),
    )
    return jax.shard_map(
        on_device, mesh=mesh, in_specs=placed, out_specs=P(("frame", "head"), None), check_vma=False
    )
```
